512 devices in a mesh: frames: 64 (over y_hi, z, core), rows: 8 (over x, y_lo).
Axes of the slice: x: 4, y: 8 (y_hi: 4, y_lo: 2; y = y_hi * 2 + y_lo), z: 8, core: 2. Of those that a mesh axis runs over, the one named last changes fastest.
Arguments:
- tokens: bfloat16 [64, 128, 16, 256], P('frames', 'rows'), may hold values from -6 to 6
- keep_mask: int32 [64, 128, 16], P('frames'), may hold values 0 or 1
- gain_two: float32 [256], replicated, may hold values from 0.1 to 1.9
- attend_two: bfloat16 [256, 768], replicated, may hold values from -0.375 to 0.375
- scale_two: float32 [4], replicated, may hold values from 2 to 8
- output_two: bfloat16 [256, 256], replicated, may hold values from -0.375 to 0.375
- merge_weight: bfloat16 [1024, 512], replicated, may hold values from -0.1875 to 0.1875
- gain_three: float32 [512], replicated, may hold values from 0.1 to 1.9
- attend_three: bfloat16 [512, 1536], replicated, may hold values from -0.25 to 0.25
- scale_three: float32 [8], replicated, may hold values from 2 to 8
- output_three: bfloat16 [512, 512], replicated, may hold values from -0.25 to 0.25
- cotangent: bfloat16 [64, 64, 8, 512], P('frames', 'rows'), may hold values from -6 to 6
Outputs:
- tokens_grad: bfloat16 [64, 128, 16, 256], P('frames', 'rows')
- weight_grads: float32 [512, 1024], P(('frames', 'rows'))
The draws below stay inside these ranges and needn't reach their ends.
Inputs may be any that keep to these rules, and one draw needn't show every extreme that they name: `keep_mask`: 1 where a patch is valid, 0 where it is padding.
All inputs are finite; a program needn't handle non-finite values. No bound on the sum of `keep_mask` on one device may be relied on, other than what follows from the above.
Results may differ from the reference program's by a relative error of at most 0.019.
Values may be sent and summed in bfloat16 or wider, within the bound.
No kernel may reach another device: no remote copies, remote signals or barrier semaphores. Data moves between devices by JAX's collectives and lax.ppermute only.
A program may use at most 64 MiB of HBM per device.

```python
import math
import jax
import jax.numpy as jnp
from jax import lax

D2 = 256
D3 = 512
HEAD = 64
COLS = 16
FRAMES = 64
NROWS = 128
HEADS2 = 4
HEADS3 = 8
GSHARD = 1024
DEVICES = 512


def set_ends(array, key, low, high):
    longest = array.shape.index(max(array.shape))
    spots = []
    for shift in (0, 1):
        where = [jax.random.randint(jax.random.fold_in(key, axis), (), 0, length) for axis, length in enumerate(array.shape)]
        where[longest] = (where[longest] + shift) % array.shape[longest]
        spots.append(tuple(where))
    return array.at[spots[0]].set(low).at[spots[1]].set(high)


def shard_levels(own_key, dims, split, low, high):
    def one(position, parts):
        heights = jax.random.uniform(jax.random.fold_in(jax.random.fold_in(own_key, 6), position), (parts,), jnp.float32, low / len(split), high / len(split))
        return jnp.repeat(jnp.exp(heights), dims[position] // parts).reshape((-1,) + (1,) * (len(dims) - position - 1))

    level = one(*split[0])
    for cut in split[1:]:
        level = level * one(*cut)
    return level


def scatter_about(stream_key, extent, deviation, limit, shards=(), held_as=jnp.bfloat16):
    values = deviation * jax.random.normal(stream_key, extent, jnp.float32)
    if shards:
        values = values * shard_levels(stream_key, extent, shards, -0.22, 0.18)
    return jnp.clip(values, -limit, limit).astype(held_as)


def setup_inputs(seed: int = 0) -> dict:
    streams_of = jax.random.split(jax.random.key(seed), 13)
    tokens = scatter_about(streams_of[0], (FRAMES, NROWS, COLS, D2), 1.0, 6.0, ((0, 64), (1, 8)))
    keep_mask = set_ends((jax.random.randint(streams_of[1], (FRAMES, NROWS, COLS), 0, 4) < 3).astype(jnp.int32), jax.random.fold_in(streams_of[1], 1), 0, 1)
    gain_two = jnp.clip(1.0 + 0.18 * jax.random.normal(streams_of[2], (D2,), jnp.float32), 0.1, 1.9)
    attend_two = scatter_about(streams_of[3], (D2, 3 * D2), D2 ** -0.5, 0.375)
    scale_two = jnp.clip(jnp.exp(jax.random.uniform(streams_of[4], (HEADS2,), jnp.float32, math.log(2.0), math.log(8.0))), 2.0, 8.0)
    output_two = scatter_about(streams_of[5], (D2, D2), D2 ** -0.5, 0.375)
    merge_weight = scatter_about(streams_of[6], (4 * D2, D3), (4 * D2) ** -0.5, 0.1875)
    gain_three = jnp.clip(1.0 + 0.18 * jax.random.normal(streams_of[7], (D3,), jnp.float32), 0.1, 1.9)
    attend_three = scatter_about(streams_of[8], (D3, 3 * D3), D3 ** -0.5, 0.25)
    scale_three = jnp.clip(jnp.exp(jax.random.uniform(streams_of[9], (HEADS3,), jnp.float32, math.log(2.0), math.log(8.0))), 2.0, 8.0)
    output_three = scatter_about(streams_of[10], (D3, D3), D3 ** -0.5, 0.25)
    cotangent = scatter_about(streams_of[11], (FRAMES, NROWS // 2, COLS // 2, D3), 1.0, 6.0, ((0, 64), (1, 8)))
    return {"tokens": tokens, "keep_mask": keep_mask, "gain_two": gain_two, "attend_two": attend_two, "scale_two": scale_two, "output_two": output_two, "merge_weight": merge_weight, "gain_three": gain_three, "attend_three": attend_three, "scale_three": scale_three, "output_three": output_three, "cotangent": cotangent}


epsilon = 1e-06

def float_dot(left, right):
    return jnp.dot(left, right, preferred_element_type=jnp.float32, precision=lax.Precision.HIGHEST)

def project(left, right):
    return float_dot(left, right).astype(jnp.bfloat16)

def scaled_norm(values, gain):
    return (values * lax.rsqrt(lax.optimization_barrier(jnp.mean(values * values, axis=-1, keepdims=True)) + epsilon) * gain).astype(jnp.bfloat16)

def cosine_heads(triple, scale, head):
    width = triple.shape[-1] // 3
    count = triple.shape[0]
    heads = width // head
    query = triple[:, :width].astype(jnp.float32).reshape(count, heads, head)
    keys = triple[:, width:2 * width].astype(jnp.float32).reshape(count, heads, head)
    query = query * lax.rsqrt(lax.optimization_barrier(jnp.sum(query * query, axis=-1, keepdims=True)) + epsilon) * scale[:, None]
    keys = keys * lax.rsqrt(lax.optimization_barrier(jnp.sum(keys * keys, axis=-1, keepdims=True)) + epsilon)
    query = query.reshape(count, width).astype(jnp.bfloat16)
    keys = keys.reshape(count, width).astype(jnp.bfloat16)
    return (query, jnp.concatenate([keys, triple[:, 2 * width:]], axis=-1))

def tile_masks():
    query_pos = jnp.arange(64)
    key_pos = jnp.arange(196)
    down = key_pos[None, :] // 14 - query_pos[:, None] // 8
    across = key_pos[None, :] % 14 - query_pos[:, None] % 8
    inside = ((down >= 0) & (down <= 6) & (across >= 0) & (across <= 6)).astype(jnp.float32)
    centre = ((down == 3) & (across == 3)).astype(jnp.float32)
    return (inside, centre)

def neighbour_attention(query, padded, allow_pad, head):
    frames, rows, cols, width = query.shape
    heads = width // head
    row_tiles = rows // 8
    col_tiles = cols // 8
    blocks = query.reshape(frames, row_tiles, 8, col_tiles, 8, heads, head)
    blocks = blocks.transpose(0, 1, 3, 5, 2, 4, 6).reshape(frames, row_tiles, col_tiles, heads, 64, head)
    windows = jnp.stack([jnp.stack([padded[:, 8 * row_tile:8 * row_tile + 14, 8 * col_tile:8 * col_tile + 14] for col_tile in range(col_tiles)], 1) for row_tile in range(row_tiles)], 1)
    allowed = jnp.stack([jnp.stack([allow_pad[:, 8 * row_tile:8 * row_tile + 14, 8 * col_tile:8 * col_tile + 14] for col_tile in range(col_tiles)], 1) for row_tile in range(row_tiles)], 1)
    allowed = allowed.reshape(frames, row_tiles, col_tiles, 1, 1, 196)
    windows = windows.reshape(frames, row_tiles, col_tiles, 196, 2, heads, head).astype(jnp.bfloat16)
    inside, centre = tile_masks()
    scores = jnp.einsum('ftcqhd,ftckhd->ftchqk', blocks.transpose(0, 1, 2, 4, 3, 5), windows[:, :, :, :, 0], preferred_element_type=jnp.float32)
    weights = jnp.exp(scores) * (inside * jnp.maximum(allowed, centre))
    probs = (weights / lax.optimization_barrier(jnp.sum(weights, axis=-1, keepdims=True))).astype(jnp.bfloat16)
    result = jnp.einsum('ftchqk,ftckhd->ftchqd', probs, windows[:, :, :, :, 1], preferred_element_type=jnp.float32)
    result = result.reshape(frames, row_tiles, col_tiles, heads, 8, 8, head).transpose(0, 1, 4, 2, 5, 3, 6)
    return result.reshape(frames, rows, cols, width).astype(jnp.bfloat16)

def frame_attention(query, keyval, head):
    frames, places, width = query.shape
    heads = width // head
    queries = query.reshape(frames, places, heads, head)
    keys = keyval[:, :, :width].reshape(frames, places, heads, head)
    values = keyval[:, :, width:].reshape(frames, places, heads, head)
    scores = jnp.einsum('flhd,glhd->lhfg', queries, keys, preferred_element_type=jnp.float32)
    weights = jnp.exp(scores)
    probs = (weights / lax.optimization_barrier(jnp.sum(weights, axis=-1, keepdims=True))).astype(jnp.bfloat16)
    result = jnp.einsum('lhfg,glhd->flhd', probs, values, preferred_element_type=jnp.float32)
    return result.reshape(frames, places, width).astype(jnp.bfloat16)

def patch_merge(grid):
    frames, rows, cols, width = grid.shape
    merged = grid.reshape(frames, rows // 2, 2, cols // 2, 2, width).transpose(0, 1, 3, 2, 4, 5)
    return merged.reshape(frames * (rows // 2) * (cols // 2), 4 * width)

def reference(tokens, keep_mask, gain_two, attend_two, scale_two, output_two, merge_weight, gain_three, attend_three, scale_three, output_three, cotangent):
    widened = tokens.astype(jnp.float32).reshape(-1, D2)
    normed_two, norm_two_back = jax.vjp(lambda value: scaled_norm(value, gain_two), widened)
    triple_two, proj_two_back = jax.vjp(lambda value: project(value, attend_two), normed_two)
    (query_two, keyval_two), heads_two_back = jax.vjp(lambda value: cosine_heads(value, scale_two, HEAD), triple_two)
    query_grid = query_two.reshape(FRAMES, NROWS, COLS, D2)
    padded = jnp.pad(keyval_two.reshape(FRAMES, NROWS, COLS, 2 * D2).astype(jnp.float32), ((0, 0), (3, 3), (3, 3), (0, 0)))
    allow_pad = jnp.pad(keep_mask.astype(jnp.float32), ((0, 0), (3, 3), (3, 3)))

    def frame_forward(items):
        return neighbour_attention(items[0][None], items[1][None], items[2][None], HEAD)[0]
    attn_two = lax.map(frame_forward, (query_grid, padded, allow_pad)).reshape(-1, D2)
    mixed_two = (widened + float_dot(attn_two, output_two)).astype(jnp.bfloat16)
    merged, merge_back = jax.vjp(lambda value: project(patch_merge(value), merge_weight), mixed_two.reshape(FRAMES, NROWS, COLS, D2))
    merged_wide = merged.astype(jnp.float32)
    normed_three, norm_three_back = jax.vjp(lambda value: scaled_norm(value, gain_three), merged_wide)
    triple_three, proj_three_back = jax.vjp(lambda value: project(value, attend_three), normed_three)
    (query_three, keyval_three), heads_three_back = jax.vjp(lambda value: cosine_heads(value, scale_three, HEAD), triple_three)
    half_rows = NROWS // 2
    half_cols = COLS // 2
    query_rows = query_three.reshape(FRAMES, half_rows, half_cols, D3).transpose(1, 0, 2, 3)
    keyval_rows = keyval_three.reshape(FRAMES, half_rows, half_cols, 2 * D3).transpose(1, 0, 2, 3)
    attn_rows = lax.map(lambda items: frame_attention(items[0], items[1], HEAD), (query_rows, keyval_rows))
    attn_three = attn_rows.transpose(1, 0, 2, 3).reshape(-1, D3)
    target = cotangent.reshape(-1, D3)
    target_wide = target.astype(jnp.float32)
    grad_out_three = float_dot(attn_three.T, target)
    ct_attn_three = jax.vjp(lambda value: float_dot(value, output_three), attn_three)[1](target_wide)[0]
    ct_rows = ct_attn_three.reshape(FRAMES, half_rows, half_cols, D3).transpose(1, 0, 2, 3)

    def rows_backward(items):
        return jax.vjp(lambda query, keyval: frame_attention(query, keyval, HEAD), items[0], items[1])[1](items[2])
    ct_query_rows, ct_keyval_rows = lax.map(rows_backward, (query_rows, keyval_rows, ct_rows))
    ct_query_three = ct_query_rows.transpose(1, 0, 2, 3).reshape(-1, D3)
    ct_keyval_three = ct_keyval_rows.transpose(1, 0, 2, 3).reshape(-1, 2 * D3)
    ct_triple_three = heads_three_back((ct_query_three, ct_keyval_three))[0]
    ct_merged_wide = target_wide + norm_three_back(proj_three_back(ct_triple_three)[0])[0]
    ct_merged = ct_merged_wide.astype(jnp.bfloat16)
    ct_mixed = merge_back(ct_merged)[0].reshape(-1, D2)
    grad_out_two = float_dot(attn_two.T, ct_mixed)
    ct_widened = ct_mixed.astype(jnp.float32)
    ct_attn_two = jax.vjp(lambda value: float_dot(value, output_two), attn_two)[1](ct_widened)[0]
    ct_attn_grid = ct_attn_two.reshape(FRAMES, NROWS, COLS, D2)

    def frame_backward(items):
        back = jax.vjp(lambda query, keyval: neighbour_attention(query[None], keyval[None], items[2][None], HEAD)[0], items[0], items[1])[1]
        return back(items[3])
    ct_query_grid, ct_padded = lax.map(frame_backward, (query_grid, padded, allow_pad, ct_attn_grid))
    ct_keyval_two = ct_padded[:, 3:NROWS + 3, 3:COLS + 3].astype(jnp.bfloat16).reshape(-1, 2 * D2)
    ct_triple_two = heads_two_back((ct_query_grid.reshape(-1, D2), ct_keyval_two))[0]
    grad_attend_two = float_dot(normed_two.T, ct_triple_two)
    ct_widened = ct_widened + norm_two_back(proj_two_back(ct_triple_two)[0])[0]
    tokens_grad = ct_widened.astype(jnp.bfloat16).reshape(FRAMES, NROWS, COLS, D2)
    flat = jnp.concatenate([grad_attend_two.reshape(-1), grad_out_two.reshape(-1), grad_out_three.reshape(-1)])
    return (tokens_grad, flat.reshape(DEVICES, GSHARD))
```

```python
import jax
import jax.numpy as jnp
from jax import lax
from jax.experimental import pallas as pl
from jax.experimental.pallas import tpu as pltpu
from jax.sharding import PartitionSpec as P

EPS = 1e-06
BF = jnp.bfloat16
F32 = jnp.float32
HALO = 48
VMEM_BYTES = 32 * 1024 * 1024


def mm(left, right):
    return lax.dot_general(left, right, (((1,), (0,)), ((), ())), preferred_element_type=F32)


def mm_nt(left, right):
    return lax.dot_general(left, right, (((1,), (1,)), ((), ())), preferred_element_type=F32)


def mm_tn(left, right):
    return lax.dot_general(left, right, (((0,), (0,)), ((), ())), preferred_element_type=F32)


def iota(shape, dim):
    return lax.broadcasted_iota(jnp.int32, shape, dim)


def zero_one(condition):
    return jnp.where(condition, 1.0, 0.0).astype(BF)


def head_block():
    return zero_one((iota((256, 256), 0) >> 6) == (iota((256, 256), 1) >> 6))


def head_sum(values, block):
    half = values.astype(BF)
    parts = [mm(half[:, at : at + 256], block) for at in range(0, values.shape[1], 256)]
    return parts[0] if len(parts) == 1 else jnp.concatenate(parts, axis=1)


def scale_lanes(scale_ref, heads):
    lane = iota((1, heads * 64), 1) >> 6
    scale = scale_ref[...]
    out = jnp.zeros((1, heads * 64), F32)
    for head in range(heads):
        out = jnp.where(lane == head, scale[:, head : head + 1], out)
    return out


def split_heads(values, heads):
    lane = iota(values.shape, 1) >> 6
    zero = jnp.zeros_like(values)
    return jnp.concatenate([jnp.where(lane == head, values, zero) for head in range(heads)], axis=0)


def join_heads(stacked, heads):
    rows = stacked.shape[0] // heads
    lane = iota((rows, stacked.shape[1]), 1) >> 6
    out = stacked[:rows]
    for head in range(1, heads):
        out = jnp.where(lane == head, stacked[head * rows : (head + 1) * rows], out)
    return out


def rms(values, gain):
    scale = lax.rsqrt(jnp.mean(values * values, axis=-1, keepdims=True) + EPS)
    return (values * scale * gain).astype(BF)


def rms_back(values, gain, ct):
    scale = lax.rsqrt(jnp.mean(values * values, axis=-1, keepdims=True) + EPS)
    ct = ct * gain
    inner = jnp.mean(ct * values, axis=-1, keepdims=True)
    return scale * ct - values * (scale * scale * scale * inner)


def unit(values, block):
    return values * lax.rsqrt(head_sum(values * values, block) + EPS)


def unit_back(values, ct, block):
    scale = lax.rsqrt(head_sum(values * values, block) + EPS)
    return scale * ct - values * (scale * scale * scale * head_sum(ct * values, block))


def ordering(size, target):
    return zero_one(iota((size, target.shape[1]), 0) == target)


def merge_order():
    patch = iota((1, 256), 1)
    group = ((patch >> 3) & 2) + (patch & 1)
    return ordering(256, (group << 6) + ((patch >> 5) << 3) + ((patch >> 1) & 7))


def bits(count):
    return count.bit_length() - 1


def lanes_to_rows(values):
    count, blocks = values.shape[0], values.shape[1] // 128
    stacked = jnp.concatenate([values[:, 128 * j : 128 * j + 128] for j in range(blocks)], axis=0)
    at = iota((1, count * blocks), 1)
    target = ((at & (count - 1)) << bits(blocks)) + (at >> bits(count))
    return mm(ordering(count * blocks, target), stacked).astype(BF)


def rows_to_lanes(values, blocks):
    total = values.shape[0]
    count = total // blocks
    at = iota((1, total), 1)
    target = ((at & (blocks - 1)) << bits(count)) + (at >> bits(blocks))
    stacked = mm(ordering(total, target), values).astype(BF)
    return jnp.concatenate([stacked[count * j : count * j + count] for j in range(blocks)], axis=1)


def fine_project(
    tokens, gain, attend, scale, normed_out, raw_query_out, raw_key_out, query_out, key_out, value_out
):
    normed = rms(tokens[...].astype(F32), gain[...])
    normed_out[...] = normed
    block = head_block()
    triple = mm(normed, attend[...]).astype(BF)
    raw_query_out[...] = triple[:, :256]
    raw_key_out[...] = triple[:, 256:512]
    query = unit(triple[:, :256].astype(F32), block) * scale_lanes(scale, 4)
    query_out[...] = query.astype(BF)
    key_out[...] = unit(triple[:, 256:512].astype(F32), block).astype(BF)
    value_out[...] = triple[:, 512:]


def allowed_tiles(rank, keep):
    cell = iota((384, 128), 0)
    pick_row = zero_one((cell >> 4) + (16 * rank[0] - 3) == iota((384, 128), 1))
    kept = mm_nt(pick_row, keep[...].astype(F32).astype(BF))
    kept = jnp.where((iota((384, 16), 0) & 15) == iota((384, 16), 1), kept, 0.0)
    kept = jnp.sum(kept, axis=1, keepdims=True)
    spot, home = iota((256, 128), 0), iota((256, 128), 1)
    down = (spot >> 4) - (home >> 4) - 3
    across = (spot & 15) - (home & 15)
    inside = jnp.where((jnp.abs(down) <= 3) & (jnp.abs(across) <= 3), 1.0, 0.0)
    centre = jnp.where((down == 0) & (across == 0), 1.0, 0.0)
    return [inside * jnp.maximum(kept[at : at + 256], centre) for at in (0, 128)]


def fine_forward(
    rank,
    above,
    below,
    query,
    own_keys,
    own_value,
    tokens,
    gain,
    attend,
    keep,
    output,
    cotangent,
    merge,
    beside_out,
    raw_out,
    key_out,
    value_out,
    prob_out,
    attn_out,
    place_out,
):
    halo = jnp.concatenate([above[...], below[...]], axis=0).astype(F32)
    normed = rms(halo, gain[...])
    beside_out[...] = normed
    beside = mm(normed, attend[:, 256:]).astype(BF)
    raw_out[...] = beside[:, :256]
    beside_keys = unit(beside[:, :256].astype(F32), head_block()).astype(BF)
    beside_value = beside[:, 256:]
    rest = jnp.zeros((32, 256), BF)
    keys = jnp.concatenate([beside_keys[:HALO], own_keys[...], beside_keys[HALO:], rest], axis=0)
    value = jnp.concatenate(
        [beside_value[:HALO], own_value[...], beside_value[HALO:], rest], axis=0
    )
    key_out[...] = keys
    value_out[...] = value
    tiles = allowed_tiles(rank, keep)
    parts = []
    for tile in range(2):
        at = 128 * tile
        allowed = jnp.concatenate([tiles[tile]] * 4, axis=1)
        score = mm_nt(keys[at : at + 256], split_heads(query[at : at + 128], 4))
        weight = jnp.exp(score) * allowed
        prob = (weight / jnp.sum(weight, axis=0, keepdims=True)).astype(BF)
        prob_out[tile] = prob
        parts.append(join_heads(mm_tn(prob, value[at : at + 256]), 4))
    attn = jnp.concatenate(parts, axis=0).astype(BF)
    attn_out[...] = attn
    mixed = (tokens[...].astype(F32) + mm(attn, output[...])).astype(BF)
    patches = mm(merge_order(), mixed).astype(BF)
    merged = mm(patches[:64], merge[:256])
    for group in range(1, 4):
        merged += mm(patches[64 * group : 64 * group + 64], merge[256 * group : 256 * group + 256])
    both = jnp.concatenate([merged.astype(BF), cotangent[...]], axis=1)
    place_out[...] = lanes_to_rows(both)


def coarse(place, gain, attend, scale, output, grad_out, back_out):
    both = rows_to_lanes(place[...], 8)
    merged, target = both[:, :512].astype(F32), both[:, 512:]
    block = head_block()
    lanes = scale_lanes(scale, 8)
    normed = rms(merged, gain[...])
    triple = mm(normed, attend[...]).astype(BF)
    query_raw, key_raw = triple[:, :512].astype(F32), triple[:, 512:1024].astype(F32)
    value = triple[:, 1024:]
    query = (unit(query_raw, block) * lanes).astype(BF)
    keys = unit(key_raw, block).astype(BF)
    query_heads = split_heads(query, 8)
    weight = jnp.exp(mm_nt(keys, query_heads))
    prob = weight / jnp.sum(weight, axis=0, keepdims=True)
    prob_half = prob.astype(BF)
    attn = join_heads(mm_tn(prob_half, value), 8).astype(BF)
    at = iota((1, 512), 1)
    slot = ((at & 1) << 8) + (((at >> 1) & 7) << 5) + (at >> 4)
    grad = mm_tn(mm_nt(attn, ordering(512, slot)).astype(BF), target).astype(BF)
    grad_out[...] = jnp.concatenate([grad[:256], grad[256:]], axis=1)
    ct_attn = mm_nt(target, output[...]).astype(BF)
    ct_heads = split_heads(ct_attn, 8)
    ct_prob = mm_nt(value, ct_heads)
    ct_score = prob * (ct_prob - jnp.sum(ct_prob * prob, axis=0, keepdims=True))
    ct_score = ct_score.astype(BF)
    ct_query = join_heads(mm_tn(ct_score, keys), 8).astype(BF).astype(F32)
    ct_key = mm(ct_score, query_heads).astype(BF).astype(F32)
    ct_value = mm(prob_half, ct_heads).astype(BF)
    ct_triple = jnp.concatenate(
        [
            unit_back(query_raw, ct_query * lanes, block).astype(BF),
            unit_back(key_raw, ct_key, block).astype(BF),
            ct_value,
        ],
        axis=1,
    )
    ct_normed = mm_nt(ct_triple, attend[...]).astype(BF).astype(F32)
    ct_merged = target.astype(F32) + rms_back(merged, gain[...], ct_normed)
    back_out[...] = lanes_to_rows(ct_merged.astype(BF))


def fine_backward(
    back,
    grad_three,
    normed,
    raw_query,
    raw_key,
    query,
    normed_beside,
    raw_beside,
    keys,
    value,
    prob,
    attn,
    scale,
    output,
    merge,
    grad_out,
    above_out,
    below_out,
    mixed_out,
    ct_query_out,
    ct_key_out,
    ct_value_out,
    pieces_left,
    pieces_right,
):
    block = head_block()
    ct_merged = rows_to_lanes(back[...], 4)
    groups = [
        mm_nt(ct_merged, merge[256 * group : 256 * group + 256]).astype(BF) for group in range(4)
    ]
    ct_mixed = mm_tn(merge_order(), jnp.concatenate(groups, axis=0)).astype(BF)
    mixed_out[...] = ct_mixed
    ct_attn = mm_nt(ct_mixed, output[...]).astype(BF)
    ct_queries, ct_keys, ct_values = [], [], []
    for tile in range(2):
        at = 128 * tile
        ct_heads = split_heads(ct_attn[at : at + 128], 4)
        query_heads = split_heads(query[at : at + 128], 4)
        prob_half = prob[tile]
        wide = prob_half.astype(F32)
        ct_prob = mm_nt(value[at : at + 256], ct_heads)
        ct_score = wide * (ct_prob - jnp.sum(ct_prob * wide, axis=0, keepdims=True))
        ct_score = ct_score.astype(BF)
        ct_queries.append(join_heads(mm_tn(ct_score, keys[at : at + 256]), 4))
        ct_keys.append(mm(ct_score, query_heads))
        ct_values.append(mm(prob_half, ct_heads))
    both = []
    for at, parts, out in ((0, ct_keys, ct_key_out), (256, ct_values, ct_value_out)):
        first, second = parts
        middle = first[128:] + second[:128]
        own = jnp.concatenate([first[HALO:128], middle, second[128 : 128 + HALO]], axis=0)
        upper, lower = first[:HALO], second[128 + HALO : 128 + 2 * HALO]
        out[...] = own.astype(BF)
        above_out[:, at : at + 256] = upper.astype(BF)
        below_out[:, at : at + 256] = lower.astype(BF)
        both.append(jnp.concatenate([own, upper, lower], axis=0))
    ct_query = jnp.concatenate(ct_queries, axis=0) * scale_lanes(scale, 4)
    ct_query = unit_back(raw_query[...].astype(F32), ct_query, block).astype(BF)
    ct_query_out[...] = ct_query
    raw_keys = jnp.concatenate([raw_key[...], raw_beside[...]], axis=0).astype(F32)
    ct_key = unit_back(raw_keys, both[0], block).astype(BF)
    normed_all = jnp.concatenate([normed[...], normed_beside[...]], axis=0)
    grads = [
        mm_tn(normed[...], ct_query),
        mm_tn(normed_all, ct_key),
        mm_tn(normed_all, both[1].astype(BF)),
    ]
    last = mm_tn(attn[...], ct_mixed)
    for half, pieces in enumerate((pieces_left, pieces_right)):
        lanes = slice(128 * half, 128 * half + 128)
        for at, grad in enumerate(grads):
            pieces[pl.ds(at, 256, stride=3), :] = grad[:, lanes]
        pieces[768:] = last[:, lanes]
        for row in range(8):
            for quarter in range(4):
                part = pieces[pl.ds(4 * row + quarter, 32, stride=32), :].astype(BF)
                at = 256 * quarter + 128 * half
                grad_out[64 * row : 64 * row + 32, at : at + 128] = part
    for row in range(8):
        grad_out[64 * row + 32 : 64 * row + 64, :] = grad_three[32 * row : 32 * row + 32]


def fine_finish(
    from_above,
    from_below,
    ct_query,
    ct_key,
    ct_value,
    raw_key,
    ct_mixed,
    tokens,
    gain,
    attend,
    tokens_out,
    done_out,
):
    above, below = from_above[...].astype(F32), from_below[...].astype(F32)

    def with_edges(own, at):
        return jnp.concatenate(
            [
                own[:HALO].astype(F32) + above[:, at : at + 256],
                own[HALO : 256 - HALO].astype(F32),
                own[256 - HALO :].astype(F32) + below[:, at : at + 256],
            ],
            axis=0,
        ).astype(BF)

    key_total = with_edges(ct_key[...], 0).astype(F32)
    value_total = with_edges(ct_value[...], 256)
    ct_key_raw = unit_back(raw_key[...].astype(F32), key_total, head_block()).astype(BF)
    ct_triple = jnp.concatenate([ct_query[...], ct_key_raw, value_total], axis=1)
    ct_normed = mm_nt(ct_triple, attend[...]).astype(BF).astype(F32)
    own = tokens[...].astype(F32)
    total = ct_mixed[...].astype(F32) + rms_back(own, gain[...], ct_normed)
    tokens_out[...] = total.astype(BF)
    done_out[...] = jnp.zeros((8, 128), F32)


def add_rows(shares, out):
    total = shares[0].astype(F32)
    for row in range(1, 8):
        total += shares[row].astype(F32)
    out[...] = lanes_to_rows(total.astype(BF))


def add_frames(shares, done, out):
    del done
    total = shares[0].astype(F32)
    for frame in range(1, 64):
        total += shares[frame].astype(F32)
    out[...] = total


class Late:
    def __init__(self, copy, ref):
        self.copy, self.ref = copy, ref

    def wait(self):
        if self.copy is not None:
            self.copy.wait()
            self.copy = None

    def __getitem__(self, index):
        self.wait()
        return self.ref[index]


def split(values, *sizes):
    out, at = [], 0
    for size in sizes:
        out.append(values[at : at + size])
        at += size
    return out


def near(shape, dtype=BF):
    return pltpu.VMEM(shape, dtype)


def call(kernel, outs, *args, smem=0, scratch=(), cost=None):
    local = pl.BlockSpec(memory_space=pltpu.VMEM)
    scalar = pl.BlockSpec(memory_space=pltpu.SMEM)
    return pl.pallas_call(
        kernel,
        out_shape=outs,
        in_specs=[scalar] * smem + [local] * (len(args) - smem),
        scratch_shapes=scratch,
        out_specs=[local] * len(outs),
        compiler_params=pltpu.CompilerParams(vmem_limit_bytes=VMEM_BYTES),
        cost_estimate=cost,
    )(*args)


def fetch_and_call(kernel, outs, used, *args, cost=None):
    count = len(args)
    local = pl.BlockSpec(memory_space=pltpu.VMEM)
    hbm = pl.BlockSpec(memory_space=pltpu.HBM)

    def run(*refs):
        sources, held, rest = refs[:count], refs[count : 2 * count], refs[2 * count :]
        sems = rest[-1]
        late = []
        for at in range(count):
            copy = pltpu.make_async_copy(sources[at], held[at], sems.at[at])
            copy.start()
            late.append(Late(copy, held[at]))
        kernel(*late[:used], *rest[:-1])
        for one in late:
            one.wait()

    return pl.pallas_call(
        run,
        out_shape=[near(arg.shape, arg.dtype) for arg in args] + outs,
        in_specs=[hbm] * count,
        out_specs=[local] * (count + len(outs)),
        scratch_shapes=[pltpu.SemaphoreType.DMA((count,))],
        compiler_params=pltpu.CompilerParams(vmem_limit_bytes=VMEM_BYTES),
        cost_estimate=cost,
    )(*[pltpu.with_memory_space_constraint(arg, pltpu.HBM) for arg in args])


def body(
    tokens,
    keep_mask,
    gain_two,
    attend_two,
    scale_two,
    output_two,
    merge_weight,
    gain_three,
    attend_three,
    scale_three,
    output_three,
    cotangent,
):
    count = lax.axis_size("rows")
    to_next = [(i, i + 1) for i in range(count - 1)]
    to_last = [(i + 1, i) for i in range(count - 1)]
    own = tokens.reshape(256, 256)
    above = lax.ppermute(own[256 - HALO :], "rows", to_next)
    below = lax.ppermute(own[:HALO], "rows", to_last)
    rank = lax.axis_index("rows").astype(jnp.int32).reshape(1)
    square = (256, 256)
    (
        (own, gain_two, attend_two, scale_two, keep, output_two, cot, merge_weight),
        (gain_three, attend_three, scale_three, output_three),
        (normed, raw_query, raw_key, query, own_keys, own_value),
    ) = split(
        fetch_and_call(
            fine_project,
            [near(square)] * 6,
            4,
            own,
            gain_two.reshape(1, 256),
            attend_two,
            scale_two.reshape(1, 4),
            keep_mask.reshape(128, 16).T,
            output_two,
            cotangent.reshape(64, 512),
            merge_weight,
            gain_three.reshape(1, 512),
            attend_three,
            scale_three.reshape(1, 8),
            output_three,
            cost=pl.CostEstimate(flops=170_000_000, bytes_accessed=5_000_000, transcendentals=0),
        ),
        8,
        4,
        6,
    )
    normed_beside, raw_beside, keys, value, prob, attn, place = call(
        fine_forward,
        [
            near((96, 256)),
            near((96, 256)),
            near((384, 256)),
            near((384, 256)),
            near((2, 256, 512)),
            near(square),
            jax.ShapeDtypeStruct((512, 128), BF),
        ],
        rank,
        above,
        below,
        query,
        own_keys,
        own_value,
        own,
        gain_two,
        attend_two,
        keep,
        output_two,
        cot,
        merge_weight,
        smem=1,
    )
    place = lax.all_to_all(place.reshape(64, 8, 128), "frames", 0, 0, tiled=True)
    grad_three, back = call(
        coarse,
        [near((256, 1024)), jax.ShapeDtypeStruct((256, 128), BF)],
        place.reshape(512, 128),
        gain_three,
        attend_three,
        scale_three,
        output_three,
    )
    back = lax.all_to_all(back.reshape(64, 4, 128), "frames", 0, 0, tiled=True)
    grads, up, down, ct_mixed, ct_query, ct_key, ct_value = call(
        fine_backward,
        [
            jax.ShapeDtypeStruct((512, 1024), BF),
            jax.ShapeDtypeStruct((HALO, 512), BF),
            jax.ShapeDtypeStruct((HALO, 512), BF),
            near(square),
            near(square),
            near(square),
            near(square),
        ],
        back.reshape(256, 128),
        grad_three,
        normed,
        raw_query,
        raw_key,
        query,
        normed_beside,
        raw_beside,
        keys,
        value,
        prob,
        attn,
        scale_two,
        output_two,
        merge_weight,
        scratch=[pltpu.VMEM((1024, 128), F32)] * 2,
    )
    from_below = lax.ppermute(up, "rows", to_last)
    from_above = lax.ppermute(down, "rows", to_next)
    tokens_grad, done = call(
        fine_finish,
        [jax.ShapeDtypeStruct(square, BF), near((8, 128), F32)],
        from_above,
        from_below,
        ct_query,
        ct_key,
        ct_value,
        raw_key,
        ct_mixed,
        own,
        gain_two,
        attend_two,
        cost=pl.CostEstimate(flops=170_000_000, bytes_accessed=2_000_000, transcendentals=0),
    )
    shares = lax.all_to_all(grads.reshape(count, 64, 1024), "rows", 0, 0, tiled=True)
    (shares,) = call(add_rows, [jax.ShapeDtypeStruct((512, 128), BF)], shares)
    shares = lax.all_to_all(shares.reshape(64, 8, 128), "frames", 0, 0, tiled=True)
    (total,) = call(add_frames, [jax.ShapeDtypeStruct((8, 128), F32)], shares, done)
    return (tokens_grad.reshape(tokens.shape), total.reshape(1, 1024))


def solution(mesh):
    return jax.shard_map(
        body,
        mesh=mesh,
        in_specs=(
            P("frames", "rows", None, None),
            P("frames", None, None),
            P(),
            P(),
            P(),
            P(),
            P(),
            P(),
            P(),
            P(),
            P(),
            P("frames", "rows", None, None),
        ),
        out_specs=(P("frames", "rows", None, None), P(("frames", "rows"), None)),
        check_vma=False,
    )
```

```python
import jax
import jax.numpy as jnp
from jax import lax
from jax.experimental import pallas as pl
from jax.experimental.pallas import tpu as pltpu
from jax.sharding import PartitionSpec as P

EPS = 1e-06
BF = jnp.bfloat16
F32 = jnp.float32
HALO = 48
VMEM_BYTES = 32 * 1024 * 1024


def mm(left, right):
    return lax.dot_general(left, right, (((1,), (0,)), ((), ())), preferred_element_type=F32)


def mm_nt(left, right):
    return lax.dot_general(left, right, (((1,), (1,)), ((), ())), preferred_element_type=F32)


def mm_tn(left, right):
    return lax.dot_general(left, right, (((0,), (0,)), ((), ())), preferred_element_type=F32)


def iota(shape, dim):
    return lax.broadcasted_iota(jnp.int32, shape, dim)


def zero_one(condition):
    return jnp.where(condition, 1.0, 0.0).astype(BF)


def head_block():
    return zero_one((iota((256, 256), 0) >> 6) == (iota((256, 256), 1) >> 6))


def head_sum(values, block):
    half = values.astype(BF)
    parts = [mm(half[:, at : at + 256], block) for at in range(0, values.shape[1], 256)]
    return parts[0] if len(parts) == 1 else jnp.concatenate(parts, axis=1)


def scale_lanes(scale_ref, heads):
    lane = iota((1, heads * 64), 1) >> 6
    scale = scale_ref[...]
    out = jnp.zeros((1, heads * 64), F32)
    for head in range(heads):
        out = jnp.where(lane == head, scale[:, head : head + 1], out)
    return out


def split_heads(values, heads):
    lane = iota(values.shape, 1) >> 6
    zero = jnp.zeros_like(values)
    return jnp.concatenate([jnp.where(lane == head, values, zero) for head in range(heads)], axis=0)


def join_heads(stacked, heads):
    rows = stacked.shape[0] // heads
    lane = iota((rows, stacked.shape[1]), 1) >> 6
    out = stacked[:rows]
    for head in range(1, heads):
        out = jnp.where(lane == head, stacked[head * rows : (head + 1) * rows], out)
    return out


def rms(values, gain):
    scale = lax.rsqrt(jnp.mean(values * values, axis=-1, keepdims=True) + EPS)
    return (values * scale * gain).astype(BF)


def rms_back(values, gain, ct):
    scale = lax.rsqrt(jnp.mean(values * values, axis=-1, keepdims=True) + EPS)
    ct = ct * gain
    inner = jnp.mean(ct * values, axis=-1, keepdims=True)
    return scale * ct - values * (scale * scale * scale * inner)


def unit(values, block):
    return values * lax.rsqrt(head_sum(values * values, block) + EPS)


def unit_back(values, ct, block):
    scale = lax.rsqrt(head_sum(values * values, block) + EPS)
    return scale * ct - values * (scale * scale * scale * head_sum(ct * values, block))


def lanes_to_rows(values, rows, base):
    count, blocks = values.shape[0], values.shape[1] // 128
    for j in range(blocks):
        rows[pl.ds(base + j, count, stride=blocks), :] = values[:, 128 * j : 128 * j + 128]


def rows_to_lanes(rows, base, count, blocks):
    parts = [rows[pl.ds(base + j, count, stride=blocks), :] for j in range(blocks)]
    return jnp.concatenate(parts, axis=1)


def merged_spots():
    return [[32 * a + 16 * (group >> 1) + (group & 1) for a in range(8)] for group in range(4)]


def split_patches(mixed, rows, base):
    for half in range(2):
        at = base + 256 * half
        rows[at : at + 256] = mixed[:, 128 * half : 128 * half + 128]
    groups = []
    for spots in merged_spots():
        halves = [
            jnp.concatenate(
                [rows[pl.ds(base + 256 * half + spot, 8, stride=2), :] for spot in spots], axis=0
            )
            for half in range(2)
        ]
        groups.append(jnp.concatenate(halves, axis=1).astype(BF))
    return groups


def join_patches(groups, rows, base):
    for spots, group in zip(merged_spots(), groups):
        for a, spot in enumerate(spots):
            for half in range(2):
                part = group[8 * a : 8 * a + 8, 128 * half : 128 * half + 128]
                rows[pl.ds(base + 256 * half + spot, 8, stride=2), :] = part
    return jnp.concatenate([rows[base : base + 256], rows[base + 256 : base + 512]], axis=1)


def fine_project(
    tokens, gain, attend, scale, normed_out, raw_query_out, raw_key_out, query_out, key_out, value_out
):
    normed = rms(tokens[...].astype(F32), gain[...])
    normed_out[...] = normed
    block = head_block()
    triple = mm(normed, attend[...]).astype(BF)
    raw_query_out[...] = triple[:, :256]
    raw_key_out[...] = triple[:, 256:512]
    query = unit(triple[:, :256].astype(F32), block) * scale_lanes(scale, 4)
    query_out[...] = query.astype(BF)
    key_out[...] = unit(triple[:, 256:512].astype(F32), block).astype(BF)
    value_out[...] = triple[:, 512:]


def allowed_tiles(rank, keep):
    cell = iota((384, 128), 0)
    pick_row = zero_one((cell >> 4) + (16 * rank[0] - 3) == iota((384, 128), 1))
    kept = mm_nt(pick_row, keep[...].astype(F32).astype(BF))
    kept = jnp.where((iota((384, 16), 0) & 15) == iota((384, 16), 1), kept, 0.0)
    kept = jnp.sum(kept, axis=1, keepdims=True)
    spot, home = iota((256, 128), 0), iota((256, 128), 1)
    down = (spot >> 4) - (home >> 4) - 3
    across = (spot & 15) - (home & 15)
    inside = jnp.where((jnp.abs(down) <= 3) & (jnp.abs(across) <= 3), 1.0, 0.0)
    centre = jnp.where((down == 0) & (across == 0), 1.0, 0.0)
    return [inside * jnp.maximum(kept[at : at + 256], centre) for at in (0, 128)]


def fine_forward(
    rank,
    core,
    above,
    below,
    query,
    own_keys,
    own_value,
    tokens,
    gain,
    attend,
    keep,
    output,
    cotangent,
    merge,
    gain_far,
    attend_far,
    scale_far,
    output_far,
    beside_out,
    raw_out,
    key_out,
    value_out,
    prob_out,
    attn_out,
    gain_out,
    attend_out,
    scale_out,
    output_out,
    place_out,
    rows,
    sems,
):
    far = (gain_far, attend_far, scale_far, output_far)
    close = (gain_out, attend_out, scale_out, output_out)
    copies = [pltpu.make_async_copy(far[at], close[at], sems.at[at]) for at in range(4)]
    for copy in copies:
        copy.start()
    del core
    halo = jnp.concatenate([above[...], below[...]], axis=0).astype(F32)
    normed = rms(halo, gain[...])
    beside_out[...] = normed
    beside = mm(normed, attend[:, 256:]).astype(BF)
    raw_out[...] = beside[:, :256]
    beside_keys = unit(beside[:, :256].astype(F32), head_block()).astype(BF)
    beside_value = beside[:, 256:]
    rest = jnp.zeros((32, 256), BF)
    keys = jnp.concatenate([beside_keys[:HALO], own_keys[...], beside_keys[HALO:], rest], axis=0)
    value = jnp.concatenate(
        [beside_value[:HALO], own_value[...], beside_value[HALO:], rest], axis=0
    )
    key_out[...] = keys
    value_out[...] = value
    tiles = allowed_tiles(rank, keep)
    parts = []
    for tile in range(2):
        at = 128 * tile
        allowed = jnp.concatenate([tiles[tile]] * 4, axis=1)
        score = mm_nt(keys[at : at + 256], split_heads(query[at : at + 128], 4))
        weight = jnp.exp(score) * allowed
        prob = (weight / jnp.sum(weight, axis=0, keepdims=True)).astype(BF)
        prob_out[tile] = prob
        parts.append(join_heads(mm_tn(prob, value[at : at + 256]), 4))
    attn = jnp.concatenate(parts, axis=0).astype(BF)
    attn_out[...] = attn
    mixed = (tokens[...].astype(F32) + mm(attn, output[...])).astype(BF)
    patches = split_patches(mixed.astype(F32), rows, 0)
    merged = mm(patches[0], merge[:256])
    for group in range(1, 4):
        merged += mm(patches[group], merge[256 * group : 256 * group + 256])
    lanes_to_rows(jnp.concatenate([merged, cotangent[...].astype(F32)], axis=1), rows, 512)
    place_out[...] = rows[512:].astype(BF)
    for copy in copies:
        copy.wait()


def coarse(place, gain, attend, scale, output, grad_out, back_out, rows, back_rows):
    rows[:512] = place[...].astype(F32)
    both = rows_to_lanes(rows, 0, 64, 8)
    merged, target = both[:, :512], both[:, 512:].astype(BF)
    block = head_block()
    lanes = scale_lanes(scale, 8)
    normed = rms(merged, gain[...])
    triple = mm(normed, attend[...]).astype(BF)
    query_raw, key_raw = triple[:, :512].astype(F32), triple[:, 512:1024].astype(F32)
    value = triple[:, 1024:]
    query = (unit(query_raw, block) * lanes).astype(BF)
    keys = unit(key_raw, block).astype(BF)
    query_heads = split_heads(query, 8)
    weight = jnp.exp(mm_nt(keys, query_heads))
    prob = weight / jnp.sum(weight, axis=0, keepdims=True)
    prob_half = prob.astype(BF)
    attn = join_heads(mm_tn(prob_half, value), 8).astype(BF)
    grad = mm_tn(attn, target)
    for part in range(4):
        rows[pl.ds(part, 512, stride=4), :] = grad[:, 128 * part : 128 * part + 128]
    grad_out[...] = rows[...].astype(BF)
    ct_attn = mm_nt(target, output[...]).astype(BF)
    ct_heads = split_heads(ct_attn, 8)
    ct_prob = mm_nt(value, ct_heads)
    ct_score = prob * (ct_prob - jnp.sum(ct_prob * prob, axis=0, keepdims=True))
    ct_score = ct_score.astype(BF)
    ct_query = join_heads(mm_tn(ct_score, keys), 8).astype(BF).astype(F32)
    ct_key = mm(ct_score, query_heads).astype(BF).astype(F32)
    ct_value = mm(prob_half, ct_heads).astype(BF)
    ct_triple = jnp.concatenate(
        [
            unit_back(query_raw, ct_query * lanes, block).astype(BF),
            unit_back(key_raw, ct_key, block).astype(BF),
            ct_value,
        ],
        axis=1,
    )
    ct_normed = mm_nt(ct_triple, attend[...]).astype(BF).astype(F32)
    ct_merged = target.astype(F32) + rms_back(merged, gain[...], ct_normed)
    lanes_to_rows(ct_merged, back_rows, 0)
    back_out[...] = back_rows[...].astype(BF)


def fine_backward(
    core,
    back,
    grad_three,
    normed,
    raw_query,
    raw_key,
    query,
    normed_beside,
    raw_beside,
    keys,
    value,
    prob,
    attn,
    scale,
    output,
    merge,
    keep_out,
    send_out,
    above_out,
    below_out,
    mixed_out,
    ct_query_out,
    ct_key_out,
    ct_value_out,
    rows,
):
    block = head_block()
    rows[:256] = back[...].astype(F32)
    ct_merged = rows_to_lanes(rows, 0, 64, 4).astype(BF)
    groups = [mm_nt(ct_merged, merge[256 * group : 256 * group + 256]) for group in range(4)]
    ct_mixed = join_patches(groups, rows, 256).astype(BF)
    mixed_out[...] = ct_mixed
    ct_attn = mm_nt(ct_mixed, output[...]).astype(BF)
    ct_queries, ct_keys, ct_values = [], [], []
    for tile in range(2):
        at = 128 * tile
        ct_heads = split_heads(ct_attn[at : at + 128], 4)
        query_heads = split_heads(query[at : at + 128], 4)
        prob_half = prob[tile]
        wide = prob_half.astype(F32)
        ct_prob = mm_nt(value[at : at + 256], ct_heads)
        ct_score = wide * (ct_prob - jnp.sum(ct_prob * wide, axis=0, keepdims=True))
        ct_score = ct_score.astype(BF)
        ct_queries.append(join_heads(mm_tn(ct_score, keys[at : at + 256]), 4))
        ct_keys.append(mm(ct_score, query_heads))
        ct_values.append(mm(prob_half, ct_heads))
    both = []
    for at, parts, out in ((0, ct_keys, ct_key_out), (256, ct_values, ct_value_out)):
        first, second = parts
        middle = first[128:] + second[:128]
        own = jnp.concatenate([first[HALO:128], middle, second[128 : 128 + HALO]], axis=0)
        upper, lower = first[:HALO], second[128 + HALO : 128 + 2 * HALO]
        out[...] = own.astype(BF)
        above_out[:, at : at + 256] = upper.astype(BF)
        below_out[:, at : at + 256] = lower.astype(BF)
        both.append(jnp.concatenate([own, upper, lower], axis=0))
    ct_query = jnp.concatenate(ct_queries, axis=0) * scale_lanes(scale, 4)
    ct_query = unit_back(raw_query[...].astype(F32), ct_query, block).astype(BF)
    ct_query_out[...] = ct_query
    raw_keys = jnp.concatenate([raw_key[...], raw_beside[...]], axis=0).astype(F32)
    ct_key = unit_back(raw_keys, both[0], block).astype(BF)
    normed_all = jnp.concatenate([normed[...], normed_beside[...]], axis=0)
    grads = [
        mm_tn(normed[...], ct_query),
        mm_tn(normed_all, ct_key),
        mm_tn(normed_all, both[1].astype(BF)),
    ]
    last = mm_tn(attn[...], ct_mixed)
    for half in range(2):
        lanes = slice(128 * half, 128 * half + 128)
        for at, grad in enumerate(grads):
            rows[pl.ds(2 * at + half, 256, stride=6), :] = grad[:, lanes]
        rows[pl.ds(1536 + half, 256, stride=2), :] = last[:, lanes]
    own_even = core[0] == 0
    for pair in range(16):
        even = rows[128 * pair : 128 * pair + 64].astype(BF)
        odd = rows[128 * pair + 64 : 128 * pair + 128].astype(BF)
        at = 64 * pair
        keep_out[at : at + 64] = jnp.where(own_even, even, odd)
        send_out[at : at + 64] = jnp.where(own_even, odd, even)
        even = grad_three[128 * pair : 128 * pair + 64]
        odd = grad_three[128 * pair + 64 : 128 * pair + 128]
        at = 1024 + 64 * pair
        keep_out[at : at + 64] = jnp.where(own_even, even, odd)
        send_out[at : at + 64] = jnp.where(own_even, odd, even)


def fine_finish(
    from_above,
    from_below,
    ct_query,
    ct_key,
    ct_value,
    raw_key,
    ct_mixed,
    tokens,
    gain,
    attend,
    tokens_out,
    done_out,
):
    above, below = from_above[...].astype(F32), from_below[...].astype(F32)

    def with_edges(own, at):
        return jnp.concatenate(
            [
                own[:HALO].astype(F32) + above[:, at : at + 256],
                own[HALO : 256 - HALO].astype(F32),
                own[256 - HALO :].astype(F32) + below[:, at : at + 256],
            ],
            axis=0,
        ).astype(BF)

    key_total = with_edges(ct_key[...], 0).astype(F32)
    value_total = with_edges(ct_value[...], 256)
    ct_key_raw = unit_back(raw_key[...].astype(F32), key_total, head_block()).astype(BF)
    ct_triple = jnp.concatenate([ct_query[...], ct_key_raw, value_total], axis=1)
    ct_normed = mm_nt(ct_triple, attend[...]).astype(BF).astype(F32)
    own = tokens[...].astype(F32)
    total = ct_mixed[...].astype(F32) + rms_back(own, gain[...], ct_normed)
    tokens_out[...] = total.astype(BF)
    done_out[...] = jnp.zeros((8, 128), F32)


def add_pair(kept, sent, out):
    out[...] = (kept[...].astype(F32) + sent[...].astype(F32)).astype(BF)


def add_all(shares, done, out):
    del done
    total = [shares[at].astype(F32) for at in range(4)]
    for device in range(4, shares.shape[0]):
        total[device % 4] += shares[device].astype(F32)
    out[...] = (total[0] + total[1]) + (total[2] + total[3])


class Late:
    def __init__(self, copy, ref):
        self.copy, self.ref = copy, ref

    def wait(self):
        if self.copy is not None:
            self.copy.wait()
            self.copy = None

    def __getitem__(self, index):
        self.wait()
        return self.ref[index]


def split(values, *sizes):
    out, at = [], 0
    for size in sizes:
        out.append(values[at : at + size])
        at += size
    return out


def near(shape, dtype=BF):
    return pltpu.VMEM(shape, dtype)


def call(kernel, outs, *args, smem=0, far=0, scratch=(), cost=None):
    close = len(args) - far
    args = list(args[:close]) + [
        pltpu.with_memory_space_constraint(arg, pltpu.HBM) for arg in args[close:]
    ]
    local = pl.BlockSpec(memory_space=pltpu.VMEM)
    hbm = pl.BlockSpec(memory_space=pltpu.HBM)
    scalar = pl.BlockSpec(memory_space=pltpu.SMEM)
    return pl.pallas_call(
        kernel,
        out_shape=outs,
        in_specs=[scalar] * smem + [local] * (close - smem) + [hbm] * far,
        scratch_shapes=scratch,
        out_specs=[local] * len(outs),
        compiler_params=pltpu.CompilerParams(vmem_limit_bytes=VMEM_BYTES),
        cost_estimate=cost,
    )(*args)


def fetch_and_call(kernel, outs, used, *args, cost=None):
    count = len(args)
    local = pl.BlockSpec(memory_space=pltpu.VMEM)
    hbm = pl.BlockSpec(memory_space=pltpu.HBM)

    def run(*refs):
        sources, held, rest = refs[:count], refs[count : 2 * count], refs[2 * count :]
        sems = rest[-1]
        late = []
        for at in range(count):
            copy = pltpu.make_async_copy(sources[at], held[at], sems.at[at])
            copy.start()
            late.append(Late(copy, held[at]))
        kernel(*late[:used], *rest[:-1])
        for one in late:
            one.wait()

    return pl.pallas_call(
        run,
        out_shape=[near(arg.shape, arg.dtype) for arg in args] + outs,
        in_specs=[hbm] * count,
        out_specs=[local] * (count + len(outs)),
        scratch_shapes=[pltpu.SemaphoreType.DMA((count,))],
        compiler_params=pltpu.CompilerParams(vmem_limit_bytes=VMEM_BYTES),
        cost_estimate=cost,
    )(*[pltpu.with_memory_space_constraint(arg, pltpu.HBM) for arg in args])


def body(
    tokens,
    keep_mask,
    gain_two,
    attend_two,
    scale_two,
    output_two,
    merge_weight,
    gain_three,
    attend_three,
    scale_three,
    output_three,
    cotangent,
):
    count = lax.axis_size("rows")
    to_next = [(i, i + 1) for i in range(count - 1)]
    to_last = [(i + 1, i) for i in range(count - 1)]
    own = tokens.reshape(256, 256)
    above = lax.ppermute(own[256 - HALO :], "rows", to_next)
    below = lax.ppermute(own[:HALO], "rows", to_last)
    rank = lax.axis_index("rows").astype(jnp.int32).reshape(1)
    core = (lax.axis_index("frames") & 1).astype(jnp.int32).reshape(1)
    square = (256, 256)
    (
        (own, gain_two, attend_two, scale_two, keep, output_two, cot, merge_weight),
        (normed, raw_query, raw_key, query, own_keys, own_value),
    ) = split(
        fetch_and_call(
            fine_project,
            [near(square)] * 6,
            4,
            own,
            gain_two.reshape(1, 256),
            attend_two,
            scale_two.reshape(1, 4),
            keep_mask.reshape(128, 16).T,
            output_two,
            cotangent.reshape(64, 512),
            merge_weight,
            cost=pl.CostEstimate(flops=170_000_000, bytes_accessed=5_000_000, transcendentals=0),
        ),
        8,
        6,
    )
    gain_three, scale_three = gain_three.reshape(1, 512), scale_three.reshape(1, 8)
    three = (gain_three, attend_three, scale_three, output_three)
    normed_beside, raw_beside, keys, value, prob, attn, *three, place = call(
        fine_forward,
        [
            near((96, 256)),
            near((96, 256)),
            near((384, 256)),
            near((384, 256)),
            near((2, 256, 512)),
            near(square),
            *[near(weight.shape, weight.dtype) for weight in three],
            jax.ShapeDtypeStruct((512, 128), BF),
        ],
        rank,
        core,
        above,
        below,
        query,
        own_keys,
        own_value,
        own,
        gain_two,
        attend_two,
        keep,
        output_two,
        cot,
        merge_weight,
        *three,
        smem=2,
        far=4,
        scratch=[pltpu.VMEM((1024, 128), F32), pltpu.SemaphoreType.DMA((4,))],
    )
    place = lax.all_to_all(place.reshape(64, 8, 128), "frames", 0, 0, tiled=True)
    grad_three, back = call(
        coarse,
        [near((2048, 128)), jax.ShapeDtypeStruct((256, 128), BF)],
        place.reshape(512, 128),
        *three,
        scratch=[pltpu.VMEM((2048, 128), F32), pltpu.VMEM((256, 128), F32)],
    )
    back = lax.all_to_all(back.reshape(64, 4, 128), "frames", 0, 0, tiled=True)
    kept, sent, up, down, ct_mixed, ct_query, ct_key, ct_value = call(
        fine_backward,
        [
            near((2048, 128)),
            jax.ShapeDtypeStruct((2048, 128), BF),
            jax.ShapeDtypeStruct((HALO, 512), BF),
            jax.ShapeDtypeStruct((HALO, 512), BF),
            near(square),
            near(square),
            near(square),
            near(square),
        ],
        core,
        back.reshape(256, 128),
        grad_three,
        normed,
        raw_query,
        raw_key,
        query,
        normed_beside,
        raw_beside,
        keys,
        value,
        prob,
        attn,
        scale_two,
        output_two,
        merge_weight,
        smem=1,
        scratch=[pltpu.VMEM((2048, 128), F32)],
    )
    pairs = [(i, i ^ 1) for i in range(lax.axis_size("frames"))]
    sent = lax.ppermute(sent, "frames", pairs)
    from_below = lax.ppermute(up, "rows", to_last)
    from_above = lax.ppermute(down, "rows", to_next)
    tokens_grad, done = call(
        fine_finish,
        [jax.ShapeDtypeStruct(square, BF), near((8, 128), F32)],
        from_above,
        from_below,
        ct_query,
        ct_key,
        ct_value,
        raw_key,
        ct_mixed,
        own,
        gain_two,
        attend_two,
        cost=pl.CostEstimate(flops=170_000_000, bytes_accessed=2_000_000, transcendentals=0),
    )
    (shares,) = call(add_pair, [jax.ShapeDtypeStruct((2048, 128), BF)], kept, sent)
    every = lax.axis_size("frames") * count
    groups = [[at for at in range(every) if at // count % 2 == own] for own in (0, 1)]
    shares = lax.all_to_all(
        shares.reshape(every // 2, 8, 128),
        ("frames", "rows"),
        0,
        0,
        tiled=True,
        axis_index_groups=groups,
    )
    (total,) = call(add_all, [jax.ShapeDtypeStruct((8, 128), F32)], shares, done)
    return (tokens_grad.reshape(tokens.shape), total.reshape(1, 1024))


def solution(mesh):
    return jax.shard_map(
        body,
        mesh=mesh,
        in_specs=(
            P("frames", "rows", None, None),
            P("frames", None, None),
            P(),
            P(),
            P(),
            P(),
            P(),
            P(),
            P(),
            P(),
            P(),
            P("frames", "rows", None, None),
        ),
        out_specs=(P("frames", "rows", None, None), P(("frames", "rows"), None)),
        check_vma=False,
    )
```

```python
import jax
import jax.numpy as jnp
from jax import lax
from jax.experimental import pallas as pl
from jax.experimental.pallas import tpu as pltpu
from jax.sharding import PartitionSpec as P

EPS = 1e-06
BF = jnp.bfloat16
F32 = jnp.float32
HALO = 48
VMEM_BYTES = 32 * 1024 * 1024


def mm(left, right):
    return lax.dot_general(left, right, (((1,), (0,)), ((), ())), preferred_element_type=F32)


def mm_nt(left, right):
    return lax.dot_general(left, right, (((1,), (1,)), ((), ())), preferred_element_type=F32)


def mm_tn(left, right):
    return lax.dot_general(left, right, (((0,), (0,)), ((), ())), preferred_element_type=F32)


def iota(shape, dim):
    return lax.broadcasted_iota(jnp.int32, shape, dim)


def zero_one(condition):
    return jnp.where(condition, 1.0, 0.0).astype(BF)


def head_block():
    return zero_one((iota((256, 256), 0) >> 6) == (iota((256, 256), 1) >> 6))


def head_sum(values, block):
    half = values.astype(BF)
    parts = [mm(half[:, at : at + 256], block) for at in range(0, values.shape[1], 256)]
    return parts[0] if len(parts) == 1 else jnp.concatenate(parts, axis=1)


def scale_lanes(scale_ref, heads):
    lane = iota((1, heads * 64), 1) >> 6
    scale = scale_ref[...]
    out = jnp.zeros((1, heads * 64), F32)
    for head in range(heads):
        out = jnp.where(lane == head, scale[:, head : head + 1], out)
    return out


def split_heads(values, heads):
    lane = iota(values.shape, 1) >> 6
    zero = jnp.zeros_like(values)
    return jnp.concatenate([jnp.where(lane == head, values, zero) for head in range(heads)], axis=0)


def join_heads(stacked, heads):
    rows = stacked.shape[0] // heads
    lane = iota((rows, stacked.shape[1]), 1) >> 6
    out = stacked[:rows]
    for head in range(1, heads):
        out = jnp.where(lane == head, stacked[head * rows : (head + 1) * rows], out)
    return out


def rms(values, gain):
    scale = lax.rsqrt(jnp.mean(values * values, axis=-1, keepdims=True) + EPS)
    return (values * scale * gain).astype(BF)


def rms_back(values, gain, ct):
    scale = lax.rsqrt(jnp.mean(values * values, axis=-1, keepdims=True) + EPS)
    ct = ct * gain
    inner = jnp.mean(ct * values, axis=-1, keepdims=True)
    return scale * ct - values * (scale * scale * scale * inner)


def unit(values, block):
    return values * lax.rsqrt(head_sum(values * values, block) + EPS)


def unit_back(values, ct, block):
    scale = lax.rsqrt(head_sum(values * values, block) + EPS)
    return scale * ct - values * (scale * scale * scale * head_sum(ct * values, block))


def ordering(size, target):
    return zero_one(iota((size, target.shape[1]), 0) == target)


def merge_order():
    patch = iota((1, 256), 1)
    group = ((patch >> 3) & 2) + (patch & 1)
    return ordering(256, (group << 6) + ((patch >> 5) << 3) + ((patch >> 1) & 7))


def bits(count):
    return count.bit_length() - 1


def lanes_to_rows_product(values):
    count, blocks = values.shape[0], values.shape[1] // 128
    stacked = jnp.concatenate([values[:, 128 * j : 128 * j + 128] for j in range(blocks)], axis=0)
    at = iota((1, count * blocks), 1)
    target = ((at & (count - 1)) << bits(blocks)) + (at >> bits(count))
    return mm(ordering(count * blocks, target), stacked).astype(BF)


def lanes_to_rows(values, rows, base):
    count, blocks = values.shape[0], values.shape[1] // 128
    for j in range(blocks):
        rows[pl.ds(base + j, count, stride=blocks), :] = values[:, 128 * j : 128 * j + 128]


def rows_to_lanes(rows, base, count, blocks):
    parts = [rows[pl.ds(base + j, count, stride=blocks), :] for j in range(blocks)]
    return jnp.concatenate(parts, axis=1)


def merged_spots():
    return [[32 * a + 16 * (group >> 1) + (group & 1) for a in range(8)] for group in range(4)]


def join_patches(groups, rows, base):
    for spots, group in zip(merged_spots(), groups):
        for a, spot in enumerate(spots):
            for half in range(2):
                part = group[8 * a : 8 * a + 8, 128 * half : 128 * half + 128]
                rows[pl.ds(base + 256 * half + spot, 8, stride=2), :] = part
    return jnp.concatenate([rows[base : base + 256], rows[base + 256 : base + 512]], axis=1)


def fine_project(
    tokens, gain, attend, scale, normed_out, raw_query_out, raw_key_out, query_out, key_out, value_out
):
    normed = rms(tokens[...].astype(F32), gain[...])
    normed_out[...] = normed
    block = head_block()
    triple = mm(normed, attend[...]).astype(BF)
    raw_query_out[...] = triple[:, :256]
    raw_key_out[...] = triple[:, 256:512]
    query = unit(triple[:, :256].astype(F32), block) * scale_lanes(scale, 4)
    query_out[...] = query.astype(BF)
    key_out[...] = unit(triple[:, 256:512].astype(F32), block).astype(BF)
    value_out[...] = triple[:, 512:]


def allowed_tiles(rank, keep):
    cell = iota((384, 128), 0)
    pick_row = zero_one((cell >> 4) + (16 * rank[0] - 3) == iota((384, 128), 1))
    kept = mm_nt(pick_row, keep[...].astype(F32).astype(BF))
    kept = jnp.where((iota((384, 16), 0) & 15) == iota((384, 16), 1), kept, 0.0)
    kept = jnp.sum(kept, axis=1, keepdims=True)
    spot, home = iota((256, 128), 0), iota((256, 128), 1)
    down = (spot >> 4) - (home >> 4) - 3
    across = (spot & 15) - (home & 15)
    inside = jnp.where((jnp.abs(down) <= 3) & (jnp.abs(across) <= 3), 1.0, 0.0)
    centre = jnp.where((down == 0) & (across == 0), 1.0, 0.0)
    return [inside * jnp.maximum(kept[at : at + 256], centre) for at in (0, 128)]


def fine_forward(
    rank,
    core,
    first,
    second,
    query,
    own_keys,
    own_value,
    tokens,
    gain,
    attend,
    keep,
    output,
    cotangent,
    merge,
    beside_out,
    raw_out,
    key_out,
    value_out,
    prob_out,
    attn_out,
    place_out,
):
    del core
    is_even = (rank[0] & 1) == 0
    above = jnp.where(is_even, second[...].astype(F32), first[...].astype(F32))
    below = jnp.where(is_even, first[...].astype(F32), second[...].astype(F32))
    halo = jnp.concatenate([above, below], axis=0)
    normed = rms(halo, gain[...])
    beside_out[...] = normed
    beside = mm(normed, attend[:, 256:]).astype(BF)
    raw_out[...] = beside[:, :256]
    beside_keys = unit(beside[:, :256].astype(F32), head_block()).astype(BF)
    beside_value = beside[:, 256:]
    rest = jnp.zeros((32, 256), BF)
    keys = jnp.concatenate([beside_keys[:HALO], own_keys[...], beside_keys[HALO:], rest], axis=0)
    value = jnp.concatenate(
        [beside_value[:HALO], own_value[...], beside_value[HALO:], rest], axis=0
    )
    key_out[...] = keys
    value_out[...] = value
    tiles = allowed_tiles(rank, keep)
    parts = []
    for tile in range(2):
        at = 128 * tile
        allowed = jnp.concatenate([tiles[tile]] * 4, axis=1)
        score = mm_nt(keys[at : at + 256], split_heads(query[at : at + 128], 4))
        weight = jnp.exp(score) * allowed
        prob = (weight / jnp.sum(weight, axis=0, keepdims=True)).astype(BF)
        prob_out[tile] = prob
        parts.append(join_heads(mm_tn(prob, value[at : at + 256]), 4))
    attn = jnp.concatenate(parts, axis=0).astype(BF)
    attn_out[...] = attn
    mixed = (tokens[...].astype(F32) + mm(attn, output[...])).astype(BF)
    patches = mm(merge_order(), mixed).astype(BF)
    merged = mm(patches[:64], merge[:256])
    for group in range(1, 4):
        merged += mm(patches[64 * group : 64 * group + 64], merge[256 * group : 256 * group + 256])
    both = jnp.concatenate([merged.astype(BF), cotangent[...]], axis=1)
    place_out[...] = lanes_to_rows_product(both)


def coarse(place, gain, attend, scale, output, grad_out, back_out, rows, back_rows):
    rows[:512] = place[...].astype(F32)
    both = rows_to_lanes(rows, 0, 64, 8)
    merged, target = both[:, :512], both[:, 512:].astype(BF)
    block = head_block()
    lanes = scale_lanes(scale, 8)
    normed = rms(merged, gain[...])
    triple = mm(normed, attend[...]).astype(BF)
    query_raw, key_raw = triple[:, :512].astype(F32), triple[:, 512:1024].astype(F32)
    value = triple[:, 1024:]
    query = (unit(query_raw, block) * lanes).astype(BF)
    keys = unit(key_raw, block).astype(BF)
    query_heads = split_heads(query, 8)
    weight = jnp.exp(mm_nt(keys, query_heads))
    prob = weight / jnp.sum(weight, axis=0, keepdims=True)
    prob_half = prob.astype(BF)
    attn = join_heads(mm_tn(prob_half, value), 8).astype(BF)
    grad = mm_tn(attn, target)
    for part in range(4):
        rows[pl.ds(part, 512, stride=4), :] = grad[:, 128 * part : 128 * part + 128]
    grad_out[...] = rows[...].astype(BF)
    ct_attn = mm_nt(target, output[...]).astype(BF)
    ct_heads = split_heads(ct_attn, 8)
    ct_prob = mm_nt(value, ct_heads)
    ct_score = prob * (ct_prob - jnp.sum(ct_prob * prob, axis=0, keepdims=True))
    ct_score = ct_score.astype(BF)
    ct_query = join_heads(mm_tn(ct_score, keys), 8).astype(BF).astype(F32)
    ct_key = mm(ct_score, query_heads).astype(BF).astype(F32)
    ct_value = mm(prob_half, ct_heads).astype(BF)
    ct_triple = jnp.concatenate(
        [
            unit_back(query_raw, ct_query * lanes, block).astype(BF),
            unit_back(key_raw, ct_key, block).astype(BF),
            ct_value,
        ],
        axis=1,
    )
    ct_normed = mm_nt(ct_triple, attend[...]).astype(BF).astype(F32)
    ct_merged = target.astype(F32) + rms_back(merged, gain[...], ct_normed)
    lanes_to_rows(ct_merged, back_rows, 0)
    back_out[...] = back_rows[...].astype(BF)


def fine_backward(
    core,
    back,
    grad_three,
    normed,
    raw_query,
    raw_key,
    query,
    normed_beside,
    raw_beside,
    keys,
    value,
    prob,
    attn,
    scale,
    output,
    merge,
    keep_out,
    send_out,
    above_out,
    below_out,
    mixed_out,
    ct_query_out,
    ct_key_out,
    ct_value_out,
    rows,
):
    block = head_block()
    rows[:256] = back[...].astype(F32)
    ct_merged = rows_to_lanes(rows, 0, 64, 4).astype(BF)
    groups = [mm_nt(ct_merged, merge[256 * group : 256 * group + 256]) for group in range(4)]
    ct_mixed = join_patches(groups, rows, 256).astype(BF)
    mixed_out[...] = ct_mixed
    ct_attn = mm_nt(ct_mixed, output[...]).astype(BF)
    ct_queries, ct_keys, ct_values = [], [], []
    for tile in range(2):
        at = 128 * tile
        ct_heads = split_heads(ct_attn[at : at + 128], 4)
        query_heads = split_heads(query[at : at + 128], 4)
        prob_half = prob[tile]
        wide = prob_half.astype(F32)
        ct_prob = mm_nt(value[at : at + 256], ct_heads)
        ct_score = wide * (ct_prob - jnp.sum(ct_prob * wide, axis=0, keepdims=True))
        ct_score = ct_score.astype(BF)
        ct_queries.append(join_heads(mm_tn(ct_score, keys[at : at + 256]), 4))
        ct_keys.append(mm(ct_score, query_heads))
        ct_values.append(mm(prob_half, ct_heads))
    both = []
    for at, parts, out in ((0, ct_keys, ct_key_out), (256, ct_values, ct_value_out)):
        first, second = parts
        middle = first[128:] + second[:128]
        own = jnp.concatenate([first[HALO:128], middle, second[128 : 128 + HALO]], axis=0)
        upper, lower = first[:HALO], second[128 + HALO : 128 + 2 * HALO]
        out[...] = own.astype(BF)
        above_out[:, at : at + 256] = upper.astype(BF)
        below_out[:, at : at + 256] = lower.astype(BF)
        both.append(jnp.concatenate([own, upper, lower], axis=0))
    ct_query = jnp.concatenate(ct_queries, axis=0) * scale_lanes(scale, 4)
    ct_query = unit_back(raw_query[...].astype(F32), ct_query, block).astype(BF)
    ct_query_out[...] = ct_query
    raw_keys = jnp.concatenate([raw_key[...], raw_beside[...]], axis=0).astype(F32)
    ct_key = unit_back(raw_keys, both[0], block).astype(BF)
    normed_all = jnp.concatenate([normed[...], normed_beside[...]], axis=0)
    grads = [
        mm_tn(normed[...], ct_query),
        mm_tn(normed_all, ct_key),
        mm_tn(normed_all, both[1].astype(BF)),
    ]
    last = mm_tn(attn[...], ct_mixed)
    for half in range(2):
        lanes = slice(128 * half, 128 * half + 128)
        for at, grad in enumerate(grads):
            rows[pl.ds(2 * at + half, 256, stride=6), :] = grad[:, lanes]
        rows[pl.ds(1536 + half, 256, stride=2), :] = last[:, lanes]
    own_even = core[0] == 0
    for pair in range(16):
        even = rows[128 * pair : 128 * pair + 64].astype(BF)
        odd = rows[128 * pair + 64 : 128 * pair + 128].astype(BF)
        at = 64 * pair
        keep_out[at : at + 64] = jnp.where(own_even, even, odd)
        send_out[at : at + 64] = jnp.where(own_even, odd, even)
        even = grad_three[128 * pair : 128 * pair + 64]
        odd = grad_three[128 * pair + 64 : 128 * pair + 128]
        at = 1024 + 64 * pair
        keep_out[at : at + 64] = jnp.where(own_even, even, odd)
        send_out[at : at + 64] = jnp.where(own_even, odd, even)


def fine_finish(
    from_above,
    from_below,
    ct_query,
    ct_key,
    ct_value,
    raw_key,
    ct_mixed,
    tokens,
    gain,
    attend,
    tokens_out,
    done_out,
):
    above, below = from_above[...].astype(F32), from_below[...].astype(F32)

    def with_edges(own, at):
        return jnp.concatenate(
            [
                own[:HALO].astype(F32) + above[:, at : at + 256],
                own[HALO : 256 - HALO].astype(F32),
                own[256 - HALO :].astype(F32) + below[:, at : at + 256],
            ],
            axis=0,
        ).astype(BF)

    key_total = with_edges(ct_key[...], 0).astype(F32)
    value_total = with_edges(ct_value[...], 256)
    ct_key_raw = unit_back(raw_key[...].astype(F32), key_total, head_block()).astype(BF)
    ct_triple = jnp.concatenate([ct_query[...], ct_key_raw, value_total], axis=1)
    ct_normed = mm_nt(ct_triple, attend[...]).astype(BF).astype(F32)
    own = tokens[...].astype(F32)
    total = ct_mixed[...].astype(F32) + rms_back(own, gain[...], ct_normed)
    tokens_out[...] = total.astype(BF)
    done_out[...] = jnp.zeros((8, 128), F32)


def add_pair(kept, sent, out):
    out[...] = (kept[...].astype(F32) + sent[...].astype(F32)).astype(BF)


def add_all(shares, done, out):
    del done
    total = [shares[at].astype(F32) for at in range(4)]
    for device in range(4, shares.shape[0]):
        total[device % 4] += shares[device].astype(F32)
    out[...] = (total[0] + total[1]) + (total[2] + total[3])


class Late:
    def __init__(self, copy, ref):
        self.copy, self.ref = copy, ref

    def wait(self):
        if self.copy is not None:
            self.copy.wait()
            self.copy = None

    def __getitem__(self, index):
        self.wait()
        return self.ref[index]


def split(values, *sizes):
    out, at = [], 0
    for size in sizes:
        out.append(values[at : at + size])
        at += size
    return out


def near(shape, dtype=BF):
    return pltpu.VMEM(shape, dtype)


def call(kernel, outs, *args, smem=0, scratch=(), cost=None):
    local = pl.BlockSpec(memory_space=pltpu.VMEM)
    scalar = pl.BlockSpec(memory_space=pltpu.SMEM)
    return pl.pallas_call(
        kernel,
        out_shape=outs,
        in_specs=[scalar] * smem + [local] * (len(args) - smem),
        scratch_shapes=scratch,
        out_specs=[local] * len(outs),
        compiler_params=pltpu.CompilerParams(vmem_limit_bytes=VMEM_BYTES),
        cost_estimate=cost,
    )(*args)


def fetch_and_call(kernel, outs, used, *args, cost=None):
    count = len(args)
    local = pl.BlockSpec(memory_space=pltpu.VMEM)
    hbm = pl.BlockSpec(memory_space=pltpu.HBM)

    def run(*refs):
        sources, held, rest = refs[:count], refs[count : 2 * count], refs[2 * count :]
        sems = rest[-1]
        late = []
        for at in range(count):
            copy = pltpu.make_async_copy(sources[at], held[at], sems.at[at])
            copy.start()
            late.append(Late(copy, held[at]))
        kernel(*late[:used], *rest[:-1])
        for one in late:
            one.wait()

    return pl.pallas_call(
        run,
        out_shape=[near(arg.shape, arg.dtype) for arg in args] + outs,
        in_specs=[hbm] * count,
        out_specs=[local] * (count + len(outs)),
        scratch_shapes=[pltpu.SemaphoreType.DMA((count,))],
        compiler_params=pltpu.CompilerParams(vmem_limit_bytes=VMEM_BYTES),
        cost_estimate=cost,
    )(*[pltpu.with_memory_space_constraint(arg, pltpu.HBM) for arg in args])


def body(
    tokens,
    keep_mask,
    gain_two,
    attend_two,
    scale_two,
    output_two,
    merge_weight,
    gain_three,
    attend_three,
    scale_three,
    output_three,
    cotangent,
):
    count = lax.axis_size("rows")
    to_next = [(i, i + 1) for i in range(count - 1)]
    to_last = [(i + 1, i) for i in range(count - 1)]
    own = tokens.reshape(256, 256)
    place = lax.axis_index("rows")
    is_even = (place & 1) == 0
    top, bottom = own[:HALO], own[256 - HALO :]
    first = lax.ppermute(
        jnp.where(is_even, bottom, top), "rows", [(at, at ^ 1) for at in range(count)]
    )
    second = lax.ppermute(
        jnp.where(is_even, top, bottom), "rows", [(at, ((at + 1) ^ 1) - 1) for at in range(1, count - 1)]
    )
    rank = lax.axis_index("rows").astype(jnp.int32).reshape(1)
    core = (lax.axis_index("frames") & 1).astype(jnp.int32).reshape(1)
    square = (256, 256)
    (
        (own, gain_two, attend_two, scale_two, keep, output_two, cot, merge_weight),
        three,
        (normed, raw_query, raw_key, query, own_keys, own_value),
    ) = split(
        fetch_and_call(
            fine_project,
            [near(square)] * 6,
            4,
            own,
            gain_two.reshape(1, 256),
            attend_two,
            scale_two.reshape(1, 4),
            keep_mask.reshape(128, 16).T,
            output_two,
            cotangent.reshape(64, 512),
            merge_weight,
            gain_three.reshape(1, 512),
            attend_three,
            scale_three.reshape(1, 8),
            output_three,
            cost=pl.CostEstimate(flops=170_000_000, bytes_accessed=5_000_000, transcendentals=0),
        ),
        8,
        4,
        6,
    )
    normed_beside, raw_beside, keys, value, prob, attn, place = call(
        fine_forward,
        [
            near((96, 256)),
            near((96, 256)),
            near((384, 256)),
            near((384, 256)),
            near((2, 256, 512)),
            near(square),
            jax.ShapeDtypeStruct((512, 128), BF),
        ],
        rank,
        core,
        first,
        second,
        query,
        own_keys,
        own_value,
        own,
        gain_two,
        attend_two,
        keep,
        output_two,
        cot,
        merge_weight,
        smem=2,
    )
    place = lax.all_to_all(place.reshape(64, 8, 128), "frames", 0, 0, tiled=True)
    grad_three, back = call(
        coarse,
        [near((2048, 128)), jax.ShapeDtypeStruct((256, 128), BF)],
        place.reshape(512, 128),
        *three,
        scratch=[pltpu.VMEM((2048, 128), F32), pltpu.VMEM((256, 128), F32)],
    )
    back = lax.all_to_all(back.reshape(64, 4, 128), "frames", 0, 0, tiled=True)
    kept, sent, up, down, ct_mixed, ct_query, ct_key, ct_value = call(
        fine_backward,
        [
            near((2048, 128)),
            jax.ShapeDtypeStruct((2048, 128), BF),
            jax.ShapeDtypeStruct((HALO, 512), BF),
            jax.ShapeDtypeStruct((HALO, 512), BF),
            near(square),
            near(square),
            near(square),
            near(square),
        ],
        core,
        back.reshape(256, 128),
        grad_three,
        normed,
        raw_query,
        raw_key,
        query,
        normed_beside,
        raw_beside,
        keys,
        value,
        prob,
        attn,
        scale_two,
        output_two,
        merge_weight,
        smem=1,
        scratch=[pltpu.VMEM((2048, 128), F32)],
    )
    pairs = [(i, i ^ 1) for i in range(lax.axis_size("frames"))]
    sent = lax.ppermute(sent, "frames", pairs)
    from_below = lax.ppermute(up, "rows", to_last)
    from_above = lax.ppermute(down, "rows", to_next)
    tokens_grad, done = call(
        fine_finish,
        [jax.ShapeDtypeStruct(square, BF), near((8, 128), F32)],
        from_above,
        from_below,
        ct_query,
        ct_key,
        ct_value,
        raw_key,
        ct_mixed,
        own,
        gain_two,
        attend_two,
        cost=pl.CostEstimate(flops=170_000_000, bytes_accessed=2_000_000, transcendentals=0),
    )
    (shares,) = call(add_pair, [jax.ShapeDtypeStruct((2048, 128), BF)], kept, sent)
    every = lax.axis_size("frames") * count
    groups = [[at for at in range(every) if at // count % 2 == own] for own in (0, 1)]
    shares = lax.all_to_all(
        shares.reshape(every // 2, 8, 128),
        ("frames", "rows"),
        0,
        0,
        tiled=True,
        axis_index_groups=groups,
    )
    (total,) = call(add_all, [jax.ShapeDtypeStruct((8, 128), F32)], shares, done)
    return (tokens_grad.reshape(tokens.shape), total.reshape(1, 1024))


def solution(mesh):
    return jax.shard_map(
        body,
        mesh=mesh,
        in_specs=(
            P("frames", "rows", None, None),
            P("frames", None, None),
            P(),
            P(),
            P(),
            P(),
            P(),
            P(),
            P(),
            P(),
            P(),
            P("frames", "rows", None, None),
        ),
        out_specs=(P("frames", "rows", None, None), P(("frames", "rows"), None)),
        check_vma=False,
    )
```

```python
import jax
import jax.numpy as jnp
from jax import lax
from jax.experimental import pallas as pl
from jax.experimental.pallas import tpu as pltpu
from jax.sharding import PartitionSpec as P

EPS = 1e-06
BF = jnp.bfloat16
F32 = jnp.float32
HALO = 48
VMEM_BYTES = 32 * 1024 * 1024


def mm(left, right):
    return lax.dot_general(left, right, (((1,), (0,)), ((), ())), preferred_element_type=F32)


def mm_nt(left, right):
    return lax.dot_general(left, right, (((1,), (1,)), ((), ())), preferred_element_type=F32)


def mm_tn(left, right):
    return lax.dot_general(left, right, (((0,), (0,)), ((), ())), preferred_element_type=F32)


def iota(shape, dim):
    return lax.broadcasted_iota(jnp.int32, shape, dim)


def zero_one(condition):
    return jnp.where(condition, 1.0, 0.0).astype(BF)


def head_block():
    return zero_one((iota((256, 256), 0) >> 6) == (iota((256, 256), 1) >> 6))


def head_sum(values, block):
    half = values.astype(BF)
    parts = [mm(half[:, at : at + 256], block) for at in range(0, values.shape[1], 256)]
    return parts[0] if len(parts) == 1 else jnp.concatenate(parts, axis=1)


def scale_lanes(scale_ref, heads):
    lane = iota((1, heads * 64), 1) >> 6
    scale = scale_ref[...]
    out = jnp.zeros((1, heads * 64), F32)
    for head in range(heads):
        out = jnp.where(lane == head, scale[:, head : head + 1], out)
    return out


def split_heads(values, heads):
    lane = iota(values.shape, 1) >> 6
    zero = jnp.zeros_like(values)
    return jnp.concatenate([jnp.where(lane == head, values, zero) for head in range(heads)], axis=0)


def join_heads(stacked, heads):
    rows = stacked.shape[0] // heads
    lane = iota((rows, stacked.shape[1]), 1) >> 6
    out = stacked[:rows]
    for head in range(1, heads):
        out = jnp.where(lane == head, stacked[head * rows : (head + 1) * rows], out)
    return out


def rms(values, gain):
    scale = lax.rsqrt(jnp.mean(values * values, axis=-1, keepdims=True) + EPS)
    return (values * scale * gain).astype(BF)


def rms_back(values, gain, ct):
    scale = lax.rsqrt(jnp.mean(values * values, axis=-1, keepdims=True) + EPS)
    ct = ct * gain
    inner = jnp.mean(ct * values, axis=-1, keepdims=True)
    return scale * ct - values * (scale * scale * scale * inner)


def unit(values, block):
    return values * lax.rsqrt(head_sum(values * values, block) + EPS)


def unit_back(values, ct, block):
    scale = lax.rsqrt(head_sum(values * values, block) + EPS)
    return scale * ct - values * (scale * scale * scale * head_sum(ct * values, block))


def ordering(size, target):
    return zero_one(iota((size, target.shape[1]), 0) == target)


def merge_order():
    patch = iota((1, 256), 1)
    group = ((patch >> 3) & 2) + (patch & 1)
    return ordering(256, (group << 6) + ((patch >> 5) << 3) + ((patch >> 1) & 7))


def bits(count):
    return count.bit_length() - 1


def lanes_to_rows(values, rows, base):
    count, blocks = values.shape[0], values.shape[1] // 128
    for j in range(blocks):
        rows[pl.ds(base + j, count, stride=blocks), :] = values[:, 128 * j : 128 * j + 128]


def rows_to_lanes(rows, base, count, blocks):
    parts = [rows[pl.ds(base + j, count, stride=blocks), :] for j in range(blocks)]
    return jnp.concatenate(parts, axis=1)


def merged_spots():
    return [[32 * a + 16 * (group >> 1) + (group & 1) for a in range(8)] for group in range(4)]


def join_patches(groups, rows, base):
    for spots, group in zip(merged_spots(), groups):
        for a, spot in enumerate(spots):
            for half in range(2):
                part = group[8 * a : 8 * a + 8, 128 * half : 128 * half + 128]
                rows[pl.ds(base + 256 * half + spot, 8, stride=2), :] = part
    return jnp.concatenate([rows[base : base + 256], rows[base + 256 : base + 512]], axis=1)


def fine_project(
    tokens, gain, attend, scale, normed_out, raw_query_out, raw_key_out, query_out, key_out, value_out
):
    normed = rms(tokens[...].astype(F32), gain[...])
    normed_out[...] = normed
    block = head_block()
    triple = mm(normed, attend[...]).astype(BF)
    raw_query_out[...] = triple[:, :256]
    raw_key_out[...] = triple[:, 256:512]
    query = unit(triple[:, :256].astype(F32), block) * scale_lanes(scale, 4)
    query_out[...] = query.astype(BF)
    key_out[...] = unit(triple[:, 256:512].astype(F32), block).astype(BF)
    value_out[...] = triple[:, 512:]


def allowed_tiles(rank, keep):
    cell = iota((384, 128), 0)
    pick_row = zero_one((cell >> 4) + (16 * rank[0] - 3) == iota((384, 128), 1))
    kept = mm_nt(pick_row, keep[...].astype(F32).astype(BF))
    kept = jnp.where((iota((384, 16), 0) & 15) == iota((384, 16), 1), kept, 0.0)
    kept = jnp.sum(kept, axis=1, keepdims=True)
    spot, home = iota((256, 128), 0), iota((256, 128), 1)
    down = (spot >> 4) - (home >> 4) - 3
    across = (spot & 15) - (home & 15)
    inside = jnp.where((jnp.abs(down) <= 3) & (jnp.abs(across) <= 3), 1.0, 0.0)
    centre = jnp.where((down == 0) & (across == 0), 1.0, 0.0)
    return [inside * jnp.maximum(kept[at : at + 256], centre) for at in (0, 128)]


def fine_forward(
    rank,
    core,
    first,
    second,
    query,
    own_keys,
    own_value,
    tokens,
    gain,
    attend,
    keep,
    output,
    cotangent,
    merge,
    beside_out,
    raw_out,
    key_out,
    value_out,
    prob_out,
    attn_out,
    place_out,
    rows,
):
    del core
    is_even = (rank[0] & 1) == 0
    above = jnp.where(is_even, second[...].astype(F32), first[...].astype(F32))
    below = jnp.where(is_even, first[...].astype(F32), second[...].astype(F32))
    halo = jnp.concatenate([above, below], axis=0)
    normed = rms(halo, gain[...])
    beside_out[...] = normed
    beside = mm(normed, attend[:, 256:]).astype(BF)
    raw_out[...] = beside[:, :256]
    beside_keys = unit(beside[:, :256].astype(F32), head_block()).astype(BF)
    beside_value = beside[:, 256:]
    rest = jnp.zeros((32, 256), BF)
    keys = jnp.concatenate([beside_keys[:HALO], own_keys[...], beside_keys[HALO:], rest], axis=0)
    value = jnp.concatenate(
        [beside_value[:HALO], own_value[...], beside_value[HALO:], rest], axis=0
    )
    key_out[...] = keys
    value_out[...] = value
    tiles = allowed_tiles(rank, keep)
    parts = []
    for tile in range(2):
        at = 128 * tile
        allowed = jnp.concatenate([tiles[tile]] * 4, axis=1)
        score = mm_nt(keys[at : at + 256], split_heads(query[at : at + 128], 4))
        weight = jnp.exp(score) * allowed
        prob = (weight / jnp.sum(weight, axis=0, keepdims=True)).astype(BF)
        prob_out[tile] = prob
        parts.append(join_heads(mm_tn(prob, value[at : at + 256]), 4))
    attn = jnp.concatenate(parts, axis=0).astype(BF)
    attn_out[...] = attn
    mixed = (tokens[...].astype(F32) + mm(attn, output[...])).astype(BF)
    patches = mm(merge_order(), mixed).astype(BF)
    merged = mm(patches[:64], merge[:256])
    for group in range(1, 4):
        merged += mm(patches[64 * group : 64 * group + 64], merge[256 * group : 256 * group + 256])
    lanes_to_rows(jnp.concatenate([merged, cotangent[...].astype(F32)], axis=1), rows, 0)
    place_out[...] = rows[...].astype(BF)


def coarse(place, gain, attend, scale, output, grad_out, back_out, rows, back_rows):
    rows[:512] = place[...].astype(F32)
    both = rows_to_lanes(rows, 0, 64, 8)
    merged, target = both[:, :512], both[:, 512:].astype(BF)
    block = head_block()
    lanes = scale_lanes(scale, 8)
    normed = rms(merged, gain[...])
    triple = mm(normed, attend[...]).astype(BF)
    query_raw, key_raw = triple[:, :512].astype(F32), triple[:, 512:1024].astype(F32)
    value = triple[:, 1024:]
    query = (unit(query_raw, block) * lanes).astype(BF)
    keys = unit(key_raw, block).astype(BF)
    ct_attn = mm_nt(target, output[...]).astype(BF)
    attns, ct_queries, ct_keys, ct_values = [], [], [], []
    for at in (0, 256):
        part = slice(at, at + 256)
        query_heads = split_heads(query[:, part], 4)
        weight = jnp.exp(mm_nt(keys[:, part], query_heads))
        prob = weight / jnp.sum(weight, axis=0, keepdims=True)
        prob_half = prob.astype(BF)
        attns.append(join_heads(mm_tn(prob_half, value[:, part]), 4).astype(BF))
        ct_heads = split_heads(ct_attn[:, part], 4)
        ct_prob = mm_nt(value[:, part], ct_heads)
        ct_score = prob * (ct_prob - jnp.sum(ct_prob * prob, axis=0, keepdims=True))
        ct_score = ct_score.astype(BF)
        ct_queries.append(join_heads(mm_tn(ct_score, keys[:, part]), 4))
        ct_keys.append(mm(ct_score, query_heads))
        ct_values.append(mm(prob_half, ct_heads))
    attn = jnp.concatenate(attns, axis=1)
    ct_query = jnp.concatenate(ct_queries, axis=1)
    ct_key = jnp.concatenate(ct_keys, axis=1)
    ct_value = jnp.concatenate(ct_values, axis=1).astype(BF)
    grad = mm_tn(attn, target)
    for part in range(4):
        rows[pl.ds(part, 512, stride=4), :] = grad[:, 128 * part : 128 * part + 128]
    grad_out[...] = rows[...].astype(BF)
    ct_triple = jnp.concatenate(
        [
            unit_back(query_raw, ct_query * lanes, block).astype(BF),
            unit_back(key_raw, ct_key, block).astype(BF),
            ct_value,
        ],
        axis=1,
    )
    ct_normed = mm_nt(ct_triple, attend[...]).astype(BF).astype(F32)
    ct_merged = target.astype(F32) + rms_back(merged, gain[...], ct_normed)
    lanes_to_rows(ct_merged, back_rows, 0)
    back_out[...] = back_rows[...].astype(BF)


def fine_backward(
    core,
    back,
    grad_three,
    normed,
    raw_query,
    raw_key,
    query,
    normed_beside,
    raw_beside,
    keys,
    value,
    prob,
    attn,
    scale,
    output,
    merge,
    keep_out,
    send_out,
    above_out,
    below_out,
    mixed_out,
    ct_query_out,
    ct_key_out,
    ct_value_out,
    rows,
):
    block = head_block()
    rows[:256] = back[...].astype(F32)
    ct_merged = rows_to_lanes(rows, 0, 64, 4).astype(BF)
    groups = [mm_nt(ct_merged, merge[256 * group : 256 * group + 256]) for group in range(4)]
    ct_mixed = join_patches(groups, rows, 256).astype(BF)
    mixed_out[...] = ct_mixed
    ct_attn = mm_nt(ct_mixed, output[...]).astype(BF)
    ct_queries, ct_keys, ct_values = [], [], []
    for tile in range(2):
        at = 128 * tile
        ct_heads = split_heads(ct_attn[at : at + 128], 4)
        query_heads = split_heads(query[at : at + 128], 4)
        prob_half = prob[tile]
        wide = prob_half.astype(F32)
        ct_prob = mm_nt(value[at : at + 256], ct_heads)
        ct_score = wide * (ct_prob - jnp.sum(ct_prob * wide, axis=0, keepdims=True))
        ct_score = ct_score.astype(BF)
        ct_queries.append(join_heads(mm_tn(ct_score, keys[at : at + 256]), 4))
        ct_keys.append(mm(ct_score, query_heads))
        ct_values.append(mm(prob_half, ct_heads))
    both = []
    for at, parts, out in ((0, ct_keys, ct_key_out), (256, ct_values, ct_value_out)):
        first, second = parts
        middle = first[128:] + second[:128]
        own = jnp.concatenate([first[HALO:128], middle, second[128 : 128 + HALO]], axis=0)
        upper, lower = first[:HALO], second[128 + HALO : 128 + 2 * HALO]
        out[...] = own.astype(BF)
        above_out[:, at : at + 256] = upper.astype(BF)
        below_out[:, at : at + 256] = lower.astype(BF)
        both.append(jnp.concatenate([own, upper, lower], axis=0))
    ct_query = jnp.concatenate(ct_queries, axis=0) * scale_lanes(scale, 4)
    ct_query = unit_back(raw_query[...].astype(F32), ct_query, block).astype(BF)
    ct_query_out[...] = ct_query
    raw_keys = jnp.concatenate([raw_key[...], raw_beside[...]], axis=0).astype(F32)
    ct_key = unit_back(raw_keys, both[0], block).astype(BF)
    normed_all = jnp.concatenate([normed[...], normed_beside[...]], axis=0)
    grads = [
        mm_tn(normed[...], ct_query),
        mm_tn(normed_all, ct_key),
        mm_tn(normed_all, both[1].astype(BF)),
    ]
    last = mm_tn(attn[...], ct_mixed)
    for half in range(2):
        lanes = slice(128 * half, 128 * half + 128)
        for at, grad in enumerate(grads):
            rows[pl.ds(2 * at + half, 256, stride=6), :] = grad[:, lanes]
        rows[pl.ds(1536 + half, 256, stride=2), :] = last[:, lanes]
    own_even = core[0] == 0
    for pair in range(16):
        even = rows[128 * pair : 128 * pair + 64].astype(BF)
        odd = rows[128 * pair + 64 : 128 * pair + 128].astype(BF)
        at = 64 * pair
        keep_out[at : at + 64] = jnp.where(own_even, even, odd)
        send_out[at : at + 64] = jnp.where(own_even, odd, even)
        even = grad_three[128 * pair : 128 * pair + 64]
        odd = grad_three[128 * pair + 64 : 128 * pair + 128]
        at = 1024 + 64 * pair
        keep_out[at : at + 64] = jnp.where(own_even, even, odd)
        send_out[at : at + 64] = jnp.where(own_even, odd, even)


def fine_finish(
    from_above,
    from_below,
    ct_query,
    ct_key,
    ct_value,
    raw_key,
    ct_mixed,
    tokens,
    gain,
    attend,
    tokens_out,
    done_out,
):
    above, below = from_above[...].astype(F32), from_below[...].astype(F32)

    def with_edges(own, at):
        return jnp.concatenate(
            [
                own[:HALO].astype(F32) + above[:, at : at + 256],
                own[HALO : 256 - HALO].astype(F32),
                own[256 - HALO :].astype(F32) + below[:, at : at + 256],
            ],
            axis=0,
        ).astype(BF)

    key_total = with_edges(ct_key[...], 0).astype(F32)
    value_total = with_edges(ct_value[...], 256)
    ct_key_raw = unit_back(raw_key[...].astype(F32), key_total, head_block()).astype(BF)
    ct_triple = jnp.concatenate([ct_query[...], ct_key_raw, value_total], axis=1)
    ct_normed = mm_nt(ct_triple, attend[...]).astype(BF).astype(F32)
    own = tokens[...].astype(F32)
    total = ct_mixed[...].astype(F32) + rms_back(own, gain[...], ct_normed)
    tokens_out[...] = total.astype(BF)
    done_out[...] = jnp.zeros((8, 128), F32)


def add_pair(kept, sent, out):
    out[...] = (kept[...].astype(F32) + sent[...].astype(F32)).astype(BF)


def add_all(shares, done, out):
    del done
    total = [shares[at].astype(F32) for at in range(4)]
    for device in range(4, shares.shape[0]):
        total[device % 4] += shares[device].astype(F32)
    out[...] = (total[0] + total[1]) + (total[2] + total[3])


class Late:
    def __init__(self, copy, ref):
        self.copy, self.ref = copy, ref

    def wait(self):
        if self.copy is not None:
            self.copy.wait()
            self.copy = None

    def __getitem__(self, index):
        self.wait()
        return self.ref[index]


def split(values, *sizes):
    out, at = [], 0
    for size in sizes:
        out.append(values[at : at + size])
        at += size
    return out


def near(shape, dtype=BF):
    return pltpu.VMEM(shape, dtype)


def call(kernel, outs, *args, smem=0, scratch=(), cost=None):
    local = pl.BlockSpec(memory_space=pltpu.VMEM)
    scalar = pl.BlockSpec(memory_space=pltpu.SMEM)
    return pl.pallas_call(
        kernel,
        out_shape=outs,
        in_specs=[scalar] * smem + [local] * (len(args) - smem),
        scratch_shapes=scratch,
        out_specs=[local] * len(outs),
        compiler_params=pltpu.CompilerParams(vmem_limit_bytes=VMEM_BYTES),
        cost_estimate=cost,
    )(*args)


def fetch_and_call(kernel, outs, used, *args, cost=None):
    count = len(args)
    local = pl.BlockSpec(memory_space=pltpu.VMEM)
    hbm = pl.BlockSpec(memory_space=pltpu.HBM)

    def run(*refs):
        sources, held, rest = refs[:count], refs[count : 2 * count], refs[2 * count :]
        sems = rest[-1]
        late = []
        for at in range(count):
            copy = pltpu.make_async_copy(sources[at], held[at], sems.at[at])
            copy.start()
            late.append(Late(copy, held[at]))
        kernel(*late[:used], *rest[:-1])
        for one in late:
            one.wait()

    return pl.pallas_call(
        run,
        out_shape=[near(arg.shape, arg.dtype) for arg in args] + outs,
        in_specs=[hbm] * count,
        out_specs=[local] * (count + len(outs)),
        scratch_shapes=[pltpu.SemaphoreType.DMA((count,))],
        compiler_params=pltpu.CompilerParams(vmem_limit_bytes=VMEM_BYTES),
        cost_estimate=cost,
    )(*[pltpu.with_memory_space_constraint(arg, pltpu.HBM) for arg in args])


def body(
    tokens,
    keep_mask,
    gain_two,
    attend_two,
    scale_two,
    output_two,
    merge_weight,
    gain_three,
    attend_three,
    scale_three,
    output_three,
    cotangent,
):
    count = lax.axis_size("rows")
    to_next = [(i, i + 1) for i in range(count - 1)]
    to_last = [(i + 1, i) for i in range(count - 1)]
    own = tokens.reshape(256, 256)
    place = lax.axis_index("rows")
    is_even = (place & 1) == 0
    top, bottom = own[:HALO], own[256 - HALO :]
    first = lax.ppermute(
        jnp.where(is_even, bottom, top), "rows", [(at, at ^ 1) for at in range(count)]
    )
    second = lax.ppermute(
        jnp.where(is_even, top, bottom), "rows", [(at, ((at + 1) ^ 1) - 1) for at in range(1, count - 1)]
    )
    rank = lax.axis_index("rows").astype(jnp.int32).reshape(1)
    core = (lax.axis_index("frames") & 1).astype(jnp.int32).reshape(1)
    square = (256, 256)
    (
        (own, gain_two, attend_two, scale_two, keep, output_two, cot, merge_weight),
        three,
        (normed, raw_query, raw_key, query, own_keys, own_value),
    ) = split(
        fetch_and_call(
            fine_project,
            [near(square)] * 6,
            4,
            own,
            gain_two.reshape(1, 256),
            attend_two,
            scale_two.reshape(1, 4),
            keep_mask.reshape(128, 16).T,
            output_two,
            cotangent.reshape(64, 512),
            merge_weight,
            gain_three.reshape(1, 512),
            attend_three,
            scale_three.reshape(1, 8),
            output_three,
            cost=pl.CostEstimate(flops=170_000_000, bytes_accessed=5_000_000, transcendentals=0),
        ),
        8,
        4,
        6,
    )
    normed_beside, raw_beside, keys, value, prob, attn, place = call(
        fine_forward,
        [
            near((96, 256)),
            near((96, 256)),
            near((384, 256)),
            near((384, 256)),
            near((2, 256, 512)),
            near(square),
            jax.ShapeDtypeStruct((512, 128), BF),
        ],
        rank,
        core,
        first,
        second,
        query,
        own_keys,
        own_value,
        own,
        gain_two,
        attend_two,
        keep,
        output_two,
        cot,
        merge_weight,
        smem=2,
        scratch=[pltpu.VMEM((512, 128), F32)],
    )
    place = lax.all_to_all(place.reshape(64, 8, 128), "frames", 0, 0, tiled=True)
    grad_three, back = call(
        coarse,
        [near((2048, 128)), jax.ShapeDtypeStruct((256, 128), BF)],
        place.reshape(512, 128),
        *three,
        scratch=[pltpu.VMEM((2048, 128), F32), pltpu.VMEM((256, 128), F32)],
    )
    back = lax.all_to_all(back.reshape(64, 4, 128), "frames", 0, 0, tiled=True)
    kept, sent, up, down, ct_mixed, ct_query, ct_key, ct_value = call(
        fine_backward,
        [
            near((2048, 128)),
            jax.ShapeDtypeStruct((2048, 128), BF),
            jax.ShapeDtypeStruct((HALO, 512), BF),
            jax.ShapeDtypeStruct((HALO, 512), BF),
            near(square),
            near(square),
            near(square),
            near(square),
        ],
        core,
        back.reshape(256, 128),
        grad_three,
        normed,
        raw_query,
        raw_key,
        query,
        normed_beside,
        raw_beside,
        keys,
        value,
        prob,
        attn,
        scale_two,
        output_two,
        merge_weight,
        smem=1,
        scratch=[pltpu.VMEM((2048, 128), F32)],
    )
    pairs = [(i, i ^ 1) for i in range(lax.axis_size("frames"))]
    sent = lax.ppermute(sent, "frames", pairs)
    from_below = lax.ppermute(up, "rows", to_last)
    from_above = lax.ppermute(down, "rows", to_next)
    tokens_grad, done = call(
        fine_finish,
        [jax.ShapeDtypeStruct(square, BF), near((8, 128), F32)],
        from_above,
        from_below,
        ct_query,
        ct_key,
        ct_value,
        raw_key,
        ct_mixed,
        own,
        gain_two,
        attend_two,
        cost=pl.CostEstimate(flops=170_000_000, bytes_accessed=2_000_000, transcendentals=0),
    )
    (shares,) = call(add_pair, [jax.ShapeDtypeStruct((2048, 128), BF)], kept, sent)
    every = lax.axis_size("frames") * count
    groups = [[at for at in range(every) if at // count % 2 == own] for own in (0, 1)]
    shares = lax.all_to_all(
        shares.reshape(every // 2, 8, 128),
        ("frames", "rows"),
        0,
        0,
        tiled=True,
        axis_index_groups=groups,
    )
    (total,) = call(add_all, [jax.ShapeDtypeStruct((8, 128), F32)], shares, done)
    return (tokens_grad.reshape(tokens.shape), total.reshape(1, 1024))


def solution(mesh):
    return jax.shard_map(
        body,
        mesh=mesh,
        in_specs=(
            P("frames", "rows", None, None),
            P("frames", None, None),
            P(),
            P(),
            P(),
            P(),
            P(),
            P(),
            P(),
            P(),
            P(),
            P("frames", "rows", None, None),
        ),
        out_specs=(P("frames", "rows", None, None), P(("frames", "rows"), None)),
        check_vma=False,
    )
```

```python
import jax
import jax.numpy as jnp
from jax import lax
from jax.experimental import pallas as pl
from jax.experimental.pallas import tpu as pltpu
from jax.sharding import PartitionSpec as P

EPS = 1e-06
BF = jnp.bfloat16
F32 = jnp.float32
HALO = 48
VMEM_BYTES = 32 * 1024 * 1024


def mm(left, right):
    return lax.dot_general(left, right, (((1,), (0,)), ((), ())), preferred_element_type=F32)


def mm_nt(left, right):
    return lax.dot_general(left, right, (((1,), (1,)), ((), ())), preferred_element_type=F32)


def mm_tn(left, right):
    return lax.dot_general(left, right, (((0,), (0,)), ((), ())), preferred_element_type=F32)


def iota(shape, dim):
    return lax.broadcasted_iota(jnp.int32, shape, dim)


def zero_one(condition):
    return jnp.where(condition, 1.0, 0.0).astype(BF)


def take_shards(rows, even_out, odd_out):
    for row in range(8):
        for z in range(8):
            for core, out in ((0, even_out), (1, odd_out)):
                first = 8 * (8 * (2 * z + core) + row)
                pair = [rows[first : first + 8], rows[1024 + first : 1024 + first + 8]]
                at = 16 * (8 * row + z)
                out[at : at + 16] = jnp.concatenate(pair, axis=0).astype(BF)


def head_block():
    return zero_one((iota((256, 256), 0) >> 6) == (iota((256, 256), 1) >> 6))


def head_sum(values, block):
    half = values.astype(BF)
    parts = [mm(half[:, at : at + 256], block) for at in range(0, values.shape[1], 256)]
    return parts[0] if len(parts) == 1 else jnp.concatenate(parts, axis=1)


def scale_lanes(scale_ref, heads):
    lane = iota((1, heads * 64), 1) >> 6
    scale = scale_ref[...]
    out = jnp.zeros((1, heads * 64), F32)
    for head in range(heads):
        out = jnp.where(lane == head, scale[:, head : head + 1], out)
    return out


def split_heads(values, heads):
    lane = iota(values.shape, 1) >> 6
    zero = jnp.zeros_like(values)
    return jnp.concatenate([jnp.where(lane == head, values, zero) for head in range(heads)], axis=0)


def join_heads(stacked, heads):
    rows = stacked.shape[0] // heads
    lane = iota((rows, stacked.shape[1]), 1) >> 6
    out = stacked[:rows]
    for head in range(1, heads):
        out = jnp.where(lane == head, stacked[head * rows : (head + 1) * rows], out)
    return out


def rms(values, gain):
    scale = lax.rsqrt(jnp.mean(values * values, axis=-1, keepdims=True) + EPS)
    return (values * scale * gain).astype(BF)


def rms_back(values, gain, ct):
    scale = lax.rsqrt(jnp.mean(values * values, axis=-1, keepdims=True) + EPS)
    ct = ct * gain
    inner = jnp.mean(ct * values, axis=-1, keepdims=True)
    return scale * ct - values * (scale * scale * scale * inner)


def unit(values, block):
    return values * lax.rsqrt(head_sum(values * values, block) + EPS)


def unit_back(values, ct, block):
    scale = lax.rsqrt(head_sum(values * values, block) + EPS)
    return scale * ct - values * (scale * scale * scale * head_sum(ct * values, block))


def ordering(size, target):
    return zero_one(iota((size, target.shape[1]), 0) == target)


def merge_order():
    patch = iota((1, 256), 1)
    group = ((patch >> 3) & 2) + (patch & 1)
    return ordering(256, (group << 6) + ((patch >> 5) << 3) + ((patch >> 1) & 7))


def bits(count):
    return count.bit_length() - 1


def lanes_to_rows(values, rows, base):
    count, blocks = values.shape[0], values.shape[1] // 128
    for j in range(blocks):
        rows[pl.ds(base + j, count, stride=blocks), :] = values[:, 128 * j : 128 * j + 128]


def rows_to_lanes(rows, base, count, blocks):
    parts = [rows[pl.ds(base + j, count, stride=blocks), :] for j in range(blocks)]
    return jnp.concatenate(parts, axis=1)


def merged_spots():
    return [[32 * a + 16 * (group >> 1) + (group & 1) for a in range(8)] for group in range(4)]


def join_patches(groups, rows, base):
    for spots, group in zip(merged_spots(), groups):
        for a, spot in enumerate(spots):
            for half in range(2):
                part = group[8 * a : 8 * a + 8, 128 * half : 128 * half + 128]
                rows[pl.ds(base + 256 * half + spot, 8, stride=2), :] = part
    return jnp.concatenate([rows[base : base + 256], rows[base + 256 : base + 512]], axis=1)


def fine_project(
    tokens, gain, attend, scale, normed_out, raw_query_out, raw_key_out, query_out, key_out, value_out
):
    normed = rms(tokens[...].astype(F32), gain[...])
    normed_out[...] = normed
    block = head_block()
    triple = mm(normed, attend[...]).astype(BF)
    raw_query_out[...] = triple[:, :256]
    raw_key_out[...] = triple[:, 256:512]
    query = unit(triple[:, :256].astype(F32), block) * scale_lanes(scale, 4)
    query_out[...] = query.astype(BF)
    key_out[...] = unit(triple[:, 256:512].astype(F32), block).astype(BF)
    value_out[...] = triple[:, 512:]


def allowed_tiles(rank, keep):
    cell = iota((384, 128), 0)
    pick_row = zero_one((cell >> 4) + (16 * rank[0] - 3) == iota((384, 128), 1))
    kept = mm_nt(pick_row, keep[...].astype(F32).astype(BF))
    kept = jnp.where((iota((384, 16), 0) & 15) == iota((384, 16), 1), kept, 0.0)
    kept = jnp.sum(kept, axis=1, keepdims=True)
    spot, home = iota((256, 128), 0), iota((256, 128), 1)
    down = (spot >> 4) - (home >> 4) - 3
    across = (spot & 15) - (home & 15)
    inside = jnp.where((jnp.abs(down) <= 3) & (jnp.abs(across) <= 3), 1.0, 0.0)
    centre = jnp.where((down == 0) & (across == 0), 1.0, 0.0)
    return [inside * jnp.maximum(kept[at : at + 256], centre) for at in (0, 128)]


def fine_forward(
    rank,
    core,
    first,
    second,
    query,
    own_keys,
    own_value,
    tokens,
    gain,
    attend,
    keep,
    output,
    cotangent,
    merge,
    beside_out,
    raw_out,
    key_out,
    value_out,
    prob_out,
    attn_out,
    place_out,
    rows,
):
    del core
    is_even = (rank[0] & 1) == 0
    above = jnp.where(is_even, second[...].astype(F32), first[...].astype(F32))
    below = jnp.where(is_even, first[...].astype(F32), second[...].astype(F32))
    halo = jnp.concatenate([above, below], axis=0)
    normed = rms(halo, gain[...])
    beside_out[...] = normed
    beside = mm(normed, attend[:, 256:]).astype(BF)
    raw_out[...] = beside[:, :256]
    beside_keys = unit(beside[:, :256].astype(F32), head_block()).astype(BF)
    beside_value = beside[:, 256:]
    rest = jnp.zeros((32, 256), BF)
    keys = jnp.concatenate([beside_keys[:HALO], own_keys[...], beside_keys[HALO:], rest], axis=0)
    value = jnp.concatenate(
        [beside_value[:HALO], own_value[...], beside_value[HALO:], rest], axis=0
    )
    key_out[...] = keys
    value_out[...] = value
    tiles = allowed_tiles(rank, keep)
    parts = []
    for tile in range(2):
        at = 128 * tile
        allowed = jnp.concatenate([tiles[tile]] * 4, axis=1)
        score = mm_nt(keys[at : at + 256], split_heads(query[at : at + 128], 4))
        weight = jnp.exp(score) * allowed
        prob = (weight / jnp.sum(weight, axis=0, keepdims=True)).astype(BF)
        prob_out[tile] = prob
        parts.append(join_heads(mm_tn(prob, value[at : at + 256]), 4))
    attn = jnp.concatenate(parts, axis=0).astype(BF)
    attn_out[...] = attn
    mixed = (tokens[...].astype(F32) + mm(attn, output[...])).astype(BF)
    patches = mm(merge_order(), mixed).astype(BF)
    merged = mm(patches[:64], merge[:256])
    for group in range(1, 4):
        merged += mm(patches[64 * group : 64 * group + 64], merge[256 * group : 256 * group + 256])
    lanes_to_rows(jnp.concatenate([merged, cotangent[...].astype(F32)], axis=1), rows, 0)
    place_out[...] = rows[...].astype(BF)


def coarse(
    place, gain, attend, scale, output, even_out, odd_out, back_out, rows, back_rows
):
    rows[:512] = place[...].astype(F32)
    both = rows_to_lanes(rows, 0, 64, 8)
    merged, target = both[:, :512], both[:, 512:].astype(BF)
    block = head_block()
    lanes = scale_lanes(scale, 8)
    normed = rms(merged, gain[...])
    triple = mm(normed, attend[...]).astype(BF)
    query_raw, key_raw = triple[:, :512].astype(F32), triple[:, 512:1024].astype(F32)
    value = triple[:, 1024:]
    query = (unit(query_raw, block) * lanes).astype(BF)
    keys = unit(key_raw, block).astype(BF)
    ct_attn = mm_nt(target, output[...]).astype(BF)
    attns, ct_queries, ct_keys, ct_values = [], [], [], []
    for at in (0, 256):
        part = slice(at, at + 256)
        query_heads = split_heads(query[:, part], 4)
        weight = jnp.exp(mm_nt(keys[:, part], query_heads))
        prob = weight / jnp.sum(weight, axis=0, keepdims=True)
        prob_half = prob.astype(BF)
        attns.append(join_heads(mm_tn(prob_half, value[:, part]), 4).astype(BF))
        ct_heads = split_heads(ct_attn[:, part], 4)
        ct_prob = mm_nt(value[:, part], ct_heads)
        ct_score = prob * (ct_prob - jnp.sum(ct_prob * prob, axis=0, keepdims=True))
        ct_score = ct_score.astype(BF)
        ct_queries.append(join_heads(mm_tn(ct_score, keys[:, part]), 4))
        ct_keys.append(mm(ct_score, query_heads))
        ct_values.append(mm(prob_half, ct_heads))
    attn = jnp.concatenate(attns, axis=1)
    ct_query = jnp.concatenate(ct_queries, axis=1)
    ct_key = jnp.concatenate(ct_keys, axis=1)
    ct_value = jnp.concatenate(ct_values, axis=1).astype(BF)
    grad = mm_tn(attn, target)
    for part in range(4):
        rows[pl.ds(part, 512, stride=4), :] = grad[:, 128 * part : 128 * part + 128]
    take_shards(rows, even_out, odd_out)
    ct_triple = jnp.concatenate(
        [
            unit_back(query_raw, ct_query * lanes, block).astype(BF),
            unit_back(key_raw, ct_key, block).astype(BF),
            ct_value,
        ],
        axis=1,
    )
    ct_normed = mm_nt(ct_triple, attend[...]).astype(BF).astype(F32)
    ct_merged = target.astype(F32) + rms_back(merged, gain[...], ct_normed)
    lanes_to_rows(ct_merged, back_rows, 0)
    back_out[...] = back_rows[...].astype(BF)


def fine_backward(
    core,
    back,
    even_three,
    odd_three,
    normed,
    raw_query,
    raw_key,
    query,
    normed_beside,
    raw_beside,
    keys,
    value,
    prob,
    attn,
    scale,
    output,
    merge,
    keep_out,
    send_out,
    above_out,
    below_out,
    mixed_out,
    ct_query_out,
    ct_key_out,
    ct_value_out,
    rows,
    even,
    odd,
):
    block = head_block()
    rows[:256] = back[...].astype(F32)
    ct_merged = rows_to_lanes(rows, 0, 64, 4).astype(BF)
    groups = [mm_nt(ct_merged, merge[256 * group : 256 * group + 256]) for group in range(4)]
    ct_mixed = join_patches(groups, rows, 256).astype(BF)
    mixed_out[...] = ct_mixed
    ct_attn = mm_nt(ct_mixed, output[...]).astype(BF)
    ct_queries, ct_keys, ct_values = [], [], []
    for tile in range(2):
        at = 128 * tile
        ct_heads = split_heads(ct_attn[at : at + 128], 4)
        query_heads = split_heads(query[at : at + 128], 4)
        prob_half = prob[tile]
        wide = prob_half.astype(F32)
        ct_prob = mm_nt(value[at : at + 256], ct_heads)
        ct_score = wide * (ct_prob - jnp.sum(ct_prob * wide, axis=0, keepdims=True))
        ct_score = ct_score.astype(BF)
        ct_queries.append(join_heads(mm_tn(ct_score, keys[at : at + 256]), 4))
        ct_keys.append(mm(ct_score, query_heads))
        ct_values.append(mm(prob_half, ct_heads))
    both = []
    for at, parts, out in ((0, ct_keys, ct_key_out), (256, ct_values, ct_value_out)):
        first, second = parts
        middle = first[128:] + second[:128]
        own = jnp.concatenate([first[HALO:128], middle, second[128 : 128 + HALO]], axis=0)
        upper, lower = first[:HALO], second[128 + HALO : 128 + 2 * HALO]
        out[...] = own.astype(BF)
        above_out[:, at : at + 256] = upper.astype(BF)
        below_out[:, at : at + 256] = lower.astype(BF)
        both.append(jnp.concatenate([own, upper, lower], axis=0))
    ct_query = jnp.concatenate(ct_queries, axis=0) * scale_lanes(scale, 4)
    ct_query = unit_back(raw_query[...].astype(F32), ct_query, block).astype(BF)
    ct_query_out[...] = ct_query
    raw_keys = jnp.concatenate([raw_key[...], raw_beside[...]], axis=0).astype(F32)
    ct_key = unit_back(raw_keys, both[0], block).astype(BF)
    normed_all = jnp.concatenate([normed[...], normed_beside[...]], axis=0)
    grads = [
        mm_tn(normed[...], ct_query),
        mm_tn(normed_all, ct_key),
        mm_tn(normed_all, both[1].astype(BF)),
    ]
    last = mm_tn(attn[...], ct_mixed)
    for half in range(2):
        lanes = slice(128 * half, 128 * half + 128)
        for at, grad in enumerate(grads):
            rows[pl.ds(2 * at + half, 256, stride=6), :] = grad[:, lanes]
        rows[pl.ds(1536 + half, 256, stride=2), :] = last[:, lanes]
    take_shards(rows, even, odd)
    own_even = core[0] == 0
    for unit_at in range(64):
        part = slice(16 * unit_at, 16 * unit_at + 16)
        at = 32 * unit_at
        for first, second in ((even[part], odd[part]), (even_three[part], odd_three[part])):
            keep_out[at : at + 16] = jnp.where(own_even, first, second)
            send_out[at : at + 16] = jnp.where(own_even, second, first)
            at += 16


def fine_finish(
    from_above,
    from_below,
    ct_query,
    ct_key,
    ct_value,
    raw_key,
    ct_mixed,
    tokens,
    gain,
    attend,
    tokens_out,
    done_out,
):
    above, below = from_above[...].astype(F32), from_below[...].astype(F32)

    def with_edges(own, at):
        return jnp.concatenate(
            [
                own[:HALO].astype(F32) + above[:, at : at + 256],
                own[HALO : 256 - HALO].astype(F32),
                own[256 - HALO :].astype(F32) + below[:, at : at + 256],
            ],
            axis=0,
        ).astype(BF)

    key_total = with_edges(ct_key[...], 0).astype(F32)
    value_total = with_edges(ct_value[...], 256)
    ct_key_raw = unit_back(raw_key[...].astype(F32), key_total, head_block()).astype(BF)
    ct_triple = jnp.concatenate([ct_query[...], ct_key_raw, value_total], axis=1)
    ct_normed = mm_nt(ct_triple, attend[...]).astype(BF).astype(F32)
    own = tokens[...].astype(F32)
    total = ct_mixed[...].astype(F32) + rms_back(own, gain[...], ct_normed)
    tokens_out[...] = total.astype(BF)
    done_out[...] = jnp.zeros((8, 128), F32)


def add_pair(kept, sent, out):
    out[...] = (kept[...].astype(F32) + sent[...].astype(F32)).astype(BF)


def add_all(shares, done, out):
    del done
    total = [shares[at].astype(F32) for at in range(4)]
    for device in range(4, shares.shape[0]):
        total[device % 4] += shares[device].astype(F32)
    out[...] = (total[0] + total[1]) + (total[2] + total[3])


class Late:
    def __init__(self, copy, ref):
        self.copy, self.ref = copy, ref

    def wait(self):
        if self.copy is not None:
            self.copy.wait()
            self.copy = None

    def __getitem__(self, index):
        self.wait()
        return self.ref[index]


def split(values, *sizes):
    out, at = [], 0
    for size in sizes:
        out.append(values[at : at + size])
        at += size
    return out


def near(shape, dtype=BF):
    return pltpu.VMEM(shape, dtype)


def call(kernel, outs, *args, smem=0, scratch=(), cost=None):
    local = pl.BlockSpec(memory_space=pltpu.VMEM)
    scalar = pl.BlockSpec(memory_space=pltpu.SMEM)
    return pl.pallas_call(
        kernel,
        out_shape=outs,
        in_specs=[scalar] * smem + [local] * (len(args) - smem),
        scratch_shapes=scratch,
        out_specs=[local] * len(outs),
        compiler_params=pltpu.CompilerParams(vmem_limit_bytes=VMEM_BYTES),
        cost_estimate=cost,
    )(*args)


def fetch_and_call(kernel, outs, used, *args, cost=None):
    count = len(args)
    local = pl.BlockSpec(memory_space=pltpu.VMEM)
    hbm = pl.BlockSpec(memory_space=pltpu.HBM)

    def run(*refs):
        sources, held, rest = refs[:count], refs[count : 2 * count], refs[2 * count :]
        sems = rest[-1]
        late = []
        for at in range(count):
            copy = pltpu.make_async_copy(sources[at], held[at], sems.at[at])
            copy.start()
            late.append(Late(copy, held[at]))
        kernel(*late[:used], *rest[:-1])
        for one in late:
            one.wait()

    return pl.pallas_call(
        run,
        out_shape=[near(arg.shape, arg.dtype) for arg in args] + outs,
        in_specs=[hbm] * count,
        out_specs=[local] * (count + len(outs)),
        scratch_shapes=[pltpu.SemaphoreType.DMA((count,))],
        compiler_params=pltpu.CompilerParams(vmem_limit_bytes=VMEM_BYTES),
        cost_estimate=cost,
    )(*[pltpu.with_memory_space_constraint(arg, pltpu.HBM) for arg in args])


def body(
    tokens,
    keep_mask,
    gain_two,
    attend_two,
    scale_two,
    output_two,
    merge_weight,
    gain_three,
    attend_three,
    scale_three,
    output_three,
    cotangent,
):
    count = lax.axis_size("rows")
    to_next = [(i, i + 1) for i in range(count - 1)]
    to_last = [(i + 1, i) for i in range(count - 1)]
    own = tokens.reshape(256, 256)
    place = lax.axis_index("rows")
    is_even = (place & 1) == 0
    top, bottom = own[:HALO], own[256 - HALO :]
    first = lax.ppermute(
        jnp.where(is_even, bottom, top), "rows", [(at, at ^ 1) for at in range(count)]
    )
    second = lax.ppermute(
        jnp.where(is_even, top, bottom), "rows", [(at, ((at + 1) ^ 1) - 1) for at in range(1, count - 1)]
    )
    rank = lax.axis_index("rows").astype(jnp.int32).reshape(1)
    core = (lax.axis_index("frames") & 1).astype(jnp.int32).reshape(1)
    square = (256, 256)
    (
        (own, gain_two, attend_two, scale_two, keep, output_two, cot, merge_weight),
        three,
        (normed, raw_query, raw_key, query, own_keys, own_value),
    ) = split(
        fetch_and_call(
            fine_project,
            [near(square)] * 6,
            4,
            own,
            gain_two.reshape(1, 256),
            attend_two,
            scale_two.reshape(1, 4),
            keep_mask.reshape(128, 16).T,
            output_two,
            cotangent.reshape(64, 512),
            merge_weight,
            gain_three.reshape(1, 512),
            attend_three,
            scale_three.reshape(1, 8),
            output_three,
            cost=pl.CostEstimate(flops=170_000_000, bytes_accessed=5_000_000, transcendentals=0),
        ),
        8,
        4,
        6,
    )
    normed_beside, raw_beside, keys, value, prob, attn, place = call(
        fine_forward,
        [
            near((96, 256)),
            near((96, 256)),
            near((384, 256)),
            near((384, 256)),
            near((2, 256, 512)),
            near(square),
            jax.ShapeDtypeStruct((512, 128), BF),
        ],
        rank,
        core,
        first,
        second,
        query,
        own_keys,
        own_value,
        own,
        gain_two,
        attend_two,
        keep,
        output_two,
        cot,
        merge_weight,
        smem=2,
        scratch=[pltpu.VMEM((512, 128), F32)],
    )
    place = lax.all_to_all(place.reshape(64, 8, 128), "frames", 0, 0, tiled=True)
    even_three, odd_three, back = call(
        coarse,
        [near((1024, 128)), near((1024, 128)), jax.ShapeDtypeStruct((256, 128), BF)],
        place.reshape(512, 128),
        *three,
        scratch=[pltpu.VMEM((2048, 128), F32), pltpu.VMEM((256, 128), F32)],
    )
    back = lax.all_to_all(back.reshape(64, 4, 128), "frames", 0, 0, tiled=True)
    kept, sent, up, down, ct_mixed, ct_query, ct_key, ct_value = call(
        fine_backward,
        [
            near((2048, 128)),
            jax.ShapeDtypeStruct((2048, 128), BF),
            jax.ShapeDtypeStruct((HALO, 512), BF),
            jax.ShapeDtypeStruct((HALO, 512), BF),
            near(square),
            near(square),
            near(square),
            near(square),
        ],
        core,
        back.reshape(256, 128),
        even_three,
        odd_three,
        normed,
        raw_query,
        raw_key,
        query,
        normed_beside,
        raw_beside,
        keys,
        value,
        prob,
        attn,
        scale_two,
        output_two,
        merge_weight,
        smem=1,
        scratch=[pltpu.VMEM((2048, 128), F32)] + [pltpu.VMEM((1024, 128), BF)] * 2,
    )
    pairs = [(i, i ^ 1) for i in range(lax.axis_size("frames"))]
    sent = lax.ppermute(sent, "frames", pairs)
    from_below = lax.ppermute(up, "rows", to_last)
    from_above = lax.ppermute(down, "rows", to_next)
    tokens_grad, done = call(
        fine_finish,
        [jax.ShapeDtypeStruct(square, BF), near((8, 128), F32)],
        from_above,
        from_below,
        ct_query,
        ct_key,
        ct_value,
        raw_key,
        ct_mixed,
        own,
        gain_two,
        attend_two,
        cost=pl.CostEstimate(flops=170_000_000, bytes_accessed=2_000_000, transcendentals=0),
    )
    (shares,) = call(add_pair, [jax.ShapeDtypeStruct((2048, 128), BF)], kept, sent)
    every = lax.axis_size("frames") * count
    groups = [
        [
            (16 * y_hi + 2 * z + own) * count + row
            for row in range(count)
            for z in range(8)
            for y_hi in range(4)
        ]
        for own in (0, 1)
    ]
    shares = lax.all_to_all(
        shares.reshape(every // 2, 8, 128),
        ("frames", "rows"),
        0,
        0,
        tiled=True,
        axis_index_groups=groups,
    )
    (total,) = call(add_all, [jax.ShapeDtypeStruct((8, 128), F32)], shares, done)
    return (tokens_grad.reshape(tokens.shape), total.reshape(1, 1024))


def solution(mesh):
    return jax.shard_map(
        body,
        mesh=mesh,
        in_specs=(
            P("frames", "rows", None, None),
            P("frames", None, None),
            P(),
            P(),
            P(),
            P(),
            P(),
            P(),
            P(),
            P(),
            P(),
            P("frames", "rows", None, None),
        ),
        out_specs=(P("frames", "rows", None, None), P(("frames", "rows"), None)),
        check_vma=False,
    )
```

```python
import jax
import jax.numpy as jnp
from jax import lax
from jax.experimental import pallas as pl
from jax.experimental.pallas import tpu as pltpu
from jax.sharding import PartitionSpec as P

EPS = 1e-06
BF = jnp.bfloat16
F32 = jnp.float32
HALO = 48
SPARE = 16
VMEM_BYTES = 32 * 1024 * 1024


def mm(left, right):
    return lax.dot_general(left, right, (((1,), (0,)), ((), ())), preferred_element_type=F32)


def mm_nt(left, right):
    return lax.dot_general(left, right, (((1,), (1,)), ((), ())), preferred_element_type=F32)


def mm_tn(left, right):
    return lax.dot_general(left, right, (((0,), (0,)), ((), ())), preferred_element_type=F32)


def iota(shape, dim):
    return lax.broadcasted_iota(jnp.int32, shape, dim)


def zero_one(condition):
    return jnp.where(condition, 1.0, 0.0).astype(BF)


def head_block():
    return zero_one((iota((256, 256), 0) >> 6) == (iota((256, 256), 1) >> 6))


def head_sum(values, block):
    half = values.astype(BF)
    parts = [mm(half[:, at : at + 256], block) for at in range(0, values.shape[1], 256)]
    return parts[0] if len(parts) == 1 else jnp.concatenate(parts, axis=1)


def scale_lanes(scale_ref, heads):
    lane = iota((1, heads * 64), 1) >> 6
    scale = scale_ref[...]
    out = jnp.zeros((1, heads * 64), F32)
    for head in range(heads):
        out = jnp.where(lane == head, scale[:, head : head + 1], out)
    return out


def split_heads(values, heads):
    lane = iota(values.shape, 1) >> 6
    zero = jnp.zeros_like(values)
    return jnp.concatenate([jnp.where(lane == head, values, zero) for head in range(heads)], axis=0)


def join_heads(stacked, heads):
    rows = stacked.shape[0] // heads
    lane = iota((rows, stacked.shape[1]), 1) >> 6
    out = stacked[:rows]
    for head in range(1, heads):
        out = jnp.where(lane == head, stacked[head * rows : (head + 1) * rows], out)
    return out


def rms(values, gain):
    scale = lax.rsqrt(jnp.mean(values * values, axis=-1, keepdims=True) + EPS)
    return (values * scale * gain).astype(BF)


def rms_back(values, gain, ct):
    scale = lax.rsqrt(jnp.mean(values * values, axis=-1, keepdims=True) + EPS)
    ct = ct * gain
    inner = jnp.mean(ct * values, axis=-1, keepdims=True)
    return scale * ct - values * (scale * scale * scale * inner)


def unit(values, block):
    return values * lax.rsqrt(head_sum(values * values, block) + EPS)


def unit_back(values, ct, block):
    scale = lax.rsqrt(head_sum(values * values, block) + EPS)
    return scale * ct - values * (scale * scale * scale * head_sum(ct * values, block))


def ordering(size, target):
    return zero_one(iota((size, target.shape[1]), 0) == target)


def merge_order():
    patch = iota((1, 256), 1)
    group = ((patch >> 3) & 2) + (patch & 1)
    return ordering(256, (group << 6) + ((patch >> 5) << 3) + ((patch >> 1) & 7))


def bits(count):
    return count.bit_length() - 1


def lanes_to_rows(values, rows, base):
    count, blocks = values.shape[0], values.shape[1] // 128
    for j in range(blocks):
        rows[pl.ds(base + j, count, stride=blocks), :] = values[:, 128 * j : 128 * j + 128]


def rows_to_lanes(rows, base, count, blocks):
    parts = [rows[pl.ds(base + j, count, stride=blocks), :] for j in range(blocks)]
    return jnp.concatenate(parts, axis=1)


def merged_spots():
    return [[32 * a + 16 * (group >> 1) + (group & 1) for a in range(8)] for group in range(4)]


def join_patches(groups, rows, base):
    for spots, group in zip(merged_spots(), groups):
        for a, spot in enumerate(spots):
            for half in range(2):
                part = group[8 * a : 8 * a + 8, 128 * half : 128 * half + 128]
                rows[pl.ds(base + 256 * half + spot, 8, stride=2), :] = part
    return jnp.concatenate([rows[base : base + 256], rows[base + 256 : base + 512]], axis=1)


def fine_project(
    tokens, gain, attend, scale, normed_out, raw_query_out, raw_key_out, query_out, key_out, value_out
):
    normed = rms(tokens[...].astype(F32), gain[...])
    normed_out[...] = normed
    block = head_block()
    triple = mm(normed, attend[...]).astype(BF)
    raw_query_out[...] = triple[:, :256]
    raw_key_out[...] = triple[:, 256:512]
    query = unit(triple[:, :256].astype(F32), block) * scale_lanes(scale, 4)
    query_out[...] = query.astype(BF)
    key_out[...] = unit(triple[:, 256:512].astype(F32), block).astype(BF)
    value_out[...] = triple[:, 512:]


def allowed_tiles(rank, keep):
    cell = iota((384, 128), 0)
    pick_row = zero_one((cell >> 4) + (16 * rank[0] - 3) == iota((384, 128), 1))
    kept = mm_nt(pick_row, keep[...].astype(F32).astype(BF))
    kept = jnp.where((iota((384, 16), 0) & 15) == iota((384, 16), 1), kept, 0.0)
    kept = jnp.sum(kept, axis=1, keepdims=True)
    spot, home = iota((256, 128), 0), iota((256, 128), 1)
    down = (spot >> 4) - (home >> 4) - 3
    across = (spot & 15) - (home & 15)
    inside = jnp.where((jnp.abs(down) <= 3) & (jnp.abs(across) <= 3), 1.0, 0.0)
    centre = jnp.where((down == 0) & (across == 0), 1.0, 0.0)
    return [inside * jnp.maximum(kept[at : at + 256], centre) for at in (0, 128)]


def fine_forward(
    rank,
    core,
    far,
    near_by,
    query,
    own_keys,
    own_value,
    tokens,
    gain,
    attend,
    keep,
    output,
    cotangent,
    merge,
    beside_out,
    raw_out,
    key_out,
    value_out,
    prob_out,
    attn_out,
    place_out,
    rows,
):
    del core
    is_even = (rank[0] & 1) == 0
    above = jnp.where(is_even, far[...].astype(F32), near_by[...].astype(F32))
    below = jnp.where(is_even, near_by[...].astype(F32), far[...].astype(F32))
    halo = jnp.concatenate([above, below], axis=0)
    normed = rms(halo, gain[...])
    beside_out[...] = normed
    beside = mm(normed, attend[:, 256:]).astype(BF)
    raw_out[...] = beside[:, :256]
    beside_keys = unit(beside[:, :256].astype(F32), head_block()).astype(BF)
    beside_value = beside[:, 256:]
    rest = jnp.zeros((32, 256), BF)
    keys = jnp.concatenate([beside_keys[:HALO], own_keys[...], beside_keys[HALO:], rest], axis=0)
    value = jnp.concatenate(
        [beside_value[:HALO], own_value[...], beside_value[HALO:], rest], axis=0
    )
    key_out[...] = keys
    value_out[...] = value
    tiles = allowed_tiles(rank, keep)
    parts = []
    for tile in range(2):
        at = 128 * tile
        allowed = jnp.concatenate([tiles[tile]] * 4, axis=1)
        score = mm_nt(keys[at : at + 256], split_heads(query[at : at + 128], 4))
        weight = jnp.exp(score) * allowed
        prob = (weight / jnp.sum(weight, axis=0, keepdims=True)).astype(BF)
        prob_out[tile] = prob
        parts.append(join_heads(mm_tn(prob, value[at : at + 256]), 4))
    attn = jnp.concatenate(parts, axis=0).astype(BF)
    attn_out[...] = attn
    mixed = (tokens[...].astype(F32) + mm(attn, output[...])).astype(BF)
    patches = mm(merge_order(), mixed).astype(BF)
    merged = mm(patches[:64], merge[:256])
    for group in range(1, 4):
        merged += mm(patches[64 * group : 64 * group + 64], merge[256 * group : 256 * group + 256])
    lanes_to_rows(jnp.concatenate([merged, cotangent[...].astype(F32)], axis=1), rows, 0)
    place_out[...] = rows[:512].astype(BF)


def coarse(place, gain, attend, scale, output, grad_out, back_out, rows, back_rows):
    rows[:512] = place[...].astype(F32)
    both = rows_to_lanes(rows, 0, 64, 8)
    merged, target = both[:, :512], both[:, 512:].astype(BF)
    block = head_block()
    lanes = scale_lanes(scale, 8)
    normed = rms(merged, gain[...])
    triple = mm(normed, attend[...]).astype(BF)
    query_raw, key_raw = triple[:, :512].astype(F32), triple[:, 512:1024].astype(F32)
    value = triple[:, 1024:]
    query = (unit(query_raw, block) * lanes).astype(BF)
    keys = unit(key_raw, block).astype(BF)
    ct_attn = mm_nt(target, output[...]).astype(BF)
    attns, ct_queries, ct_keys, ct_values = [], [], [], []
    for at in (0, 256):
        part = slice(at, at + 256)
        query_heads = split_heads(query[:, part], 4)
        weight = jnp.exp(mm_nt(keys[:, part], query_heads))
        prob = weight / jnp.sum(weight, axis=0, keepdims=True)
        prob_half = prob.astype(BF)
        attns.append(join_heads(mm_tn(prob_half, value[:, part]), 4).astype(BF))
        ct_heads = split_heads(ct_attn[:, part], 4)
        ct_prob = mm_nt(value[:, part], ct_heads)
        ct_score = prob * (ct_prob - jnp.sum(ct_prob * prob, axis=0, keepdims=True))
        ct_score = ct_score.astype(BF)
        ct_queries.append(join_heads(mm_tn(ct_score, keys[:, part]), 4))
        ct_keys.append(mm(ct_score, query_heads))
        ct_values.append(mm(prob_half, ct_heads))
    attn = jnp.concatenate(attns, axis=1)
    ct_query = jnp.concatenate(ct_queries, axis=1)
    ct_key = jnp.concatenate(ct_keys, axis=1)
    ct_value = jnp.concatenate(ct_values, axis=1).astype(BF)
    grad = mm_tn(attn, target)
    for part in range(4):
        rows[pl.ds(part, 512, stride=4), :] = grad[:, 128 * part : 128 * part + 128]
    grad_out[...] = rows[:2048].astype(BF)
    ct_triple = jnp.concatenate(
        [
            unit_back(query_raw, ct_query * lanes, block).astype(BF),
            unit_back(key_raw, ct_key, block).astype(BF),
            ct_value,
        ],
        axis=1,
    )
    ct_normed = mm_nt(ct_triple, attend[...]).astype(BF).astype(F32)
    ct_merged = target.astype(F32) + rms_back(merged, gain[...], ct_normed)
    lanes_to_rows(ct_merged, back_rows, 0)
    back_out[...] = back_rows[:256].astype(BF)


def fine_backward(
    core,
    back,
    grad_three,
    normed,
    raw_query,
    raw_key,
    query,
    normed_beside,
    raw_beside,
    keys,
    value,
    prob,
    attn,
    scale,
    output,
    merge,
    keep_out,
    send_out,
    above_out,
    below_out,
    mixed_out,
    ct_query_out,
    ct_key_out,
    ct_value_out,
    rows,
):
    block = head_block()
    rows[:256] = back[...].astype(F32)
    ct_merged = rows_to_lanes(rows, 0, 64, 4).astype(BF)
    groups = [mm_nt(ct_merged, merge[256 * group : 256 * group + 256]) for group in range(4)]
    ct_mixed = join_patches(groups, rows, 256).astype(BF)
    mixed_out[...] = ct_mixed
    ct_attn = mm_nt(ct_mixed, output[...]).astype(BF)
    ct_queries, ct_keys, ct_values = [], [], []
    for tile in range(2):
        at = 128 * tile
        ct_heads = split_heads(ct_attn[at : at + 128], 4)
        query_heads = split_heads(query[at : at + 128], 4)
        prob_half = prob[tile]
        wide = prob_half.astype(F32)
        ct_prob = mm_nt(value[at : at + 256], ct_heads)
        ct_score = wide * (ct_prob - jnp.sum(ct_prob * wide, axis=0, keepdims=True))
        ct_score = ct_score.astype(BF)
        ct_queries.append(join_heads(mm_tn(ct_score, keys[at : at + 256]), 4))
        ct_keys.append(mm(ct_score, query_heads))
        ct_values.append(mm(prob_half, ct_heads))
    both = []
    for at, parts, out in ((0, ct_keys, ct_key_out), (256, ct_values, ct_value_out)):
        first, second = parts
        middle = first[128:] + second[:128]
        own = jnp.concatenate([first[HALO:128], middle, second[128 : 128 + HALO]], axis=0)
        upper, lower = first[:HALO], second[128 + HALO : 128 + 2 * HALO]
        out[...] = own.astype(BF)
        above_out[:, at : at + 256] = upper.astype(BF)
        below_out[:, at : at + 256] = lower.astype(BF)
        both.append(jnp.concatenate([own, upper, lower], axis=0))
    ct_query = jnp.concatenate(ct_queries, axis=0) * scale_lanes(scale, 4)
    ct_query = unit_back(raw_query[...].astype(F32), ct_query, block).astype(BF)
    ct_query_out[...] = ct_query
    raw_keys = jnp.concatenate([raw_key[...], raw_beside[...]], axis=0).astype(F32)
    ct_key = unit_back(raw_keys, both[0], block).astype(BF)
    normed_all = jnp.concatenate([normed[...], normed_beside[...]], axis=0)
    grads = [
        mm_tn(normed[...], ct_query),
        mm_tn(normed_all, ct_key),
        mm_tn(normed_all, both[1].astype(BF)),
    ]
    last = mm_tn(attn[...], ct_mixed)
    for half in range(2):
        lanes = slice(128 * half, 128 * half + 128)
        for at, grad in enumerate(grads):
            rows[pl.ds(2 * at + half, 256, stride=6), :] = grad[:, lanes]
        rows[pl.ds(1536 + half, 256, stride=2), :] = last[:, lanes]
    own_even = core[0] == 0
    for pair in range(16):
        even = rows[128 * pair : 128 * pair + 64].astype(BF)
        odd = rows[128 * pair + 64 : 128 * pair + 128].astype(BF)
        at = 64 * pair
        keep_out[at : at + 64] = jnp.where(own_even, even, odd)
        send_out[at : at + 64] = jnp.where(own_even, odd, even)
        even = grad_three[128 * pair : 128 * pair + 64]
        odd = grad_three[128 * pair + 64 : 128 * pair + 128]
        at = 1024 + 64 * pair
        keep_out[at : at + 64] = jnp.where(own_even, even, odd)
        send_out[at : at + 64] = jnp.where(own_even, odd, even)


def fine_finish(
    from_above,
    from_below,
    ct_query,
    ct_key,
    ct_value,
    raw_key,
    ct_mixed,
    tokens,
    gain,
    attend,
    tokens_out,
    done_out,
):
    above, below = from_above[...].astype(F32), from_below[...].astype(F32)

    def with_edges(own, at):
        return jnp.concatenate(
            [
                own[:HALO].astype(F32) + above[:, at : at + 256],
                own[HALO : 256 - HALO].astype(F32),
                own[256 - HALO :].astype(F32) + below[:, at : at + 256],
            ],
            axis=0,
        ).astype(BF)

    key_total = with_edges(ct_key[...], 0).astype(F32)
    value_total = with_edges(ct_value[...], 256)
    ct_key_raw = unit_back(raw_key[...].astype(F32), key_total, head_block()).astype(BF)
    ct_triple = jnp.concatenate([ct_query[...], ct_key_raw, value_total], axis=1)
    ct_normed = mm_nt(ct_triple, attend[...]).astype(BF).astype(F32)
    own = tokens[...].astype(F32)
    total = ct_mixed[...].astype(F32) + rms_back(own, gain[...], ct_normed)
    tokens_out[...] = total.astype(BF)
    done_out[...] = jnp.zeros((8, 128), F32)


def add_pair(kept, sent, out):
    out[...] = (kept[...].astype(F32) + sent[...].astype(F32)).astype(BF)


def add_all(shares, done, out):
    del done
    total = [shares[at].astype(F32) for at in range(4)]
    for device in range(4, shares.shape[0]):
        total[device % 4] += shares[device].astype(F32)
    out[...] = (total[0] + total[1]) + (total[2] + total[3])


class Late:
    def __init__(self, copy, ref):
        self.copy, self.ref = copy, ref

    def wait(self):
        if self.copy is not None:
            self.copy.wait()
            self.copy = None

    def __getitem__(self, index):
        self.wait()
        return self.ref[index]


def split(values, *sizes):
    out, at = [], 0
    for size in sizes:
        out.append(values[at : at + size])
        at += size
    return out


def near(shape, dtype=BF):
    return pltpu.VMEM(shape, dtype)


def call(kernel, outs, *args, smem=0, scratch=(), cost=None):
    local = pl.BlockSpec(memory_space=pltpu.VMEM)
    scalar = pl.BlockSpec(memory_space=pltpu.SMEM)
    return pl.pallas_call(
        kernel,
        out_shape=outs,
        in_specs=[scalar] * smem + [local] * (len(args) - smem),
        scratch_shapes=scratch,
        out_specs=[local] * len(outs),
        compiler_params=pltpu.CompilerParams(vmem_limit_bytes=VMEM_BYTES),
        cost_estimate=cost,
    )(*args)


def fetch_and_call(kernel, outs, used, *args, cost=None):
    count = len(args)
    local = pl.BlockSpec(memory_space=pltpu.VMEM)
    hbm = pl.BlockSpec(memory_space=pltpu.HBM)

    def run(*refs):
        sources, held, rest = refs[:count], refs[count : 2 * count], refs[2 * count :]
        sems = rest[-1]
        late = []
        for at in range(count):
            copy = pltpu.make_async_copy(sources[at], held[at], sems.at[at])
            copy.start()
            late.append(Late(copy, held[at]))
        kernel(*late[:used], *rest[:-1])
        for one in late:
            one.wait()

    return pl.pallas_call(
        run,
        out_shape=[near(arg.shape, arg.dtype) for arg in args] + outs,
        in_specs=[hbm] * count,
        out_specs=[local] * (count + len(outs)),
        scratch_shapes=[pltpu.SemaphoreType.DMA((count,))],
        compiler_params=pltpu.CompilerParams(vmem_limit_bytes=VMEM_BYTES),
        cost_estimate=cost,
    )(*[pltpu.with_memory_space_constraint(arg, pltpu.HBM) for arg in args])


def body(
    tokens,
    keep_mask,
    gain_two,
    attend_two,
    scale_two,
    output_two,
    merge_weight,
    gain_three,
    attend_three,
    scale_three,
    output_three,
    cotangent,
):
    count = lax.axis_size("rows")
    to_next = [(i, i + 1) for i in range(count - 1)]
    to_last = [(i + 1, i) for i in range(count - 1)]
    own = tokens.reshape(256, 256)
    is_even = (lax.axis_index("rows") & 1) == 0
    top, bottom = own[:HALO], own[256 - HALO :]
    pairs = [(at, ((at + 1) ^ 1) - 1) for at in range(1, count - 1)]
    far = lax.ppermute(jnp.where(is_even, top, bottom), "rows", pairs)
    pairs = [(at, at ^ 1) for at in range(count)]
    near_by = lax.ppermute(jnp.where(is_even, bottom, top), "rows", pairs)
    rank = lax.axis_index("rows").astype(jnp.int32).reshape(1)
    core = (lax.axis_index("frames") & 1).astype(jnp.int32).reshape(1)
    square = (256, 256)
    (
        (own, gain_two, attend_two, scale_two, keep, output_two, cot, merge_weight),
        three,
        (normed, raw_query, raw_key, query, own_keys, own_value),
    ) = split(
        fetch_and_call(
            fine_project,
            [near(square)] * 6,
            4,
            own,
            gain_two.reshape(1, 256),
            attend_two,
            scale_two.reshape(1, 4),
            keep_mask.reshape(128, 16).T,
            output_two,
            cotangent.reshape(64, 512),
            merge_weight,
            gain_three.reshape(1, 512),
            attend_three,
            scale_three.reshape(1, 8),
            output_three,
            cost=pl.CostEstimate(flops=170_000_000, bytes_accessed=5_000_000, transcendentals=0),
        ),
        8,
        4,
        6,
    )
    normed_beside, raw_beside, keys, value, prob, attn, place = call(
        fine_forward,
        [
            near((96, 256)),
            near((96, 256)),
            near((384, 256)),
            near((384, 256)),
            near((2, 256, 512)),
            near(square),
            jax.ShapeDtypeStruct((512, 128), BF),
        ],
        rank,
        core,
        far,
        near_by,
        query,
        own_keys,
        own_value,
        own,
        gain_two,
        attend_two,
        keep,
        output_two,
        cot,
        merge_weight,
        smem=2,
        scratch=[pltpu.VMEM((512 + SPARE, 128), F32)],
    )
    place = lax.all_to_all(place.reshape(64, 8, 128), "frames", 0, 0, tiled=True)
    grad_three, back = call(
        coarse,
        [near((2048, 128)), jax.ShapeDtypeStruct((256, 128), BF)],
        place.reshape(512, 128),
        *three,
        scratch=[pltpu.VMEM((2048 + SPARE, 128), F32), pltpu.VMEM((256 + SPARE, 128), F32)],
    )
    back = lax.all_to_all(back.reshape(64, 4, 128), "frames", 0, 0, tiled=True)
    kept, sent, up, down, ct_mixed, ct_query, ct_key, ct_value = call(
        fine_backward,
        [
            near((2048, 128)),
            jax.ShapeDtypeStruct((2048, 128), BF),
            jax.ShapeDtypeStruct((HALO, 512), BF),
            jax.ShapeDtypeStruct((HALO, 512), BF),
            near(square),
            near(square),
            near(square),
            near(square),
        ],
        core,
        back.reshape(256, 128),
        grad_three,
        normed,
        raw_query,
        raw_key,
        query,
        normed_beside,
        raw_beside,
        keys,
        value,
        prob,
        attn,
        scale_two,
        output_two,
        merge_weight,
        smem=1,
        scratch=[pltpu.VMEM((2048 + SPARE, 128), F32)],
    )
    pairs = [(i, i ^ 1) for i in range(lax.axis_size("frames"))]
    sent = lax.ppermute(sent, "frames", pairs)
    from_below = lax.ppermute(up, "rows", to_last)
    from_above = lax.ppermute(down, "rows", to_next)
    tokens_grad, done = call(
        fine_finish,
        [jax.ShapeDtypeStruct(square, BF), near((8, 128), F32)],
        from_above,
        from_below,
        ct_query,
        ct_key,
        ct_value,
        raw_key,
        ct_mixed,
        own,
        gain_two,
        attend_two,
        cost=pl.CostEstimate(flops=170_000_000, bytes_accessed=2_000_000, transcendentals=0),
    )
    (shares,) = call(add_pair, [jax.ShapeDtypeStruct((2048, 128), BF)], kept, sent)
    every = lax.axis_size("frames") * count
    groups = [[at for at in range(every) if at // count % 2 == own] for own in (0, 1)]
    shares = lax.all_to_all(
        shares.reshape(every // 2, 8, 128),
        ("frames", "rows"),
        0,
        0,
        tiled=True,
        axis_index_groups=groups,
    )
    (total,) = call(add_all, [jax.ShapeDtypeStruct((8, 128), F32)], shares, done)
    return (tokens_grad.reshape(tokens.shape), total.reshape(1, 1024))


def solution(mesh):
    return jax.shard_map(
        body,
        mesh=mesh,
        in_specs=(
            P("frames", "rows", None, None),
            P("frames", None, None),
            P(),
            P(),
            P(),
            P(),
            P(),
            P(),
            P(),
            P(),
            P(),
            P("frames", "rows", None, None),
        ),
        out_specs=(P("frames", "rows", None, None), P(("frames", "rows"), None)),
        check_vma=False,
    )
```

```python
import jax
import jax.numpy as jnp
from jax import lax
from jax.experimental import pallas as pl
from jax.experimental.pallas import tpu as pltpu
from jax.sharding import PartitionSpec as P

EPS = 1e-06
BF = jnp.bfloat16
F32 = jnp.float32
HALO = 48
SPARE = 16
VMEM_BYTES = 32 * 1024 * 1024


def mm(left, right):
    return lax.dot_general(left, right, (((1,), (0,)), ((), ())), preferred_element_type=F32)


def mm_nt(left, right):
    return lax.dot_general(left, right, (((1,), (1,)), ((), ())), preferred_element_type=F32)


def mm_tn(left, right):
    return lax.dot_general(left, right, (((0,), (0,)), ((), ())), preferred_element_type=F32)


def iota(shape, dim):
    return lax.broadcasted_iota(jnp.int32, shape, dim)


def zero_one(condition):
    return jnp.where(condition, 1.0, 0.0).astype(BF)


def head_block():
    return zero_one((iota((256, 256), 0) >> 6) == (iota((256, 256), 1) >> 6))


def head_sum(values, block):
    half = values.astype(BF)
    parts = [mm(half[:, at : at + 256], block) for at in range(0, values.shape[1], 256)]
    return parts[0] if len(parts) == 1 else jnp.concatenate(parts, axis=1)


def scale_lanes(scale_ref, heads):
    lane = iota((1, heads * 64), 1) >> 6
    scale = scale_ref[...]
    out = jnp.zeros((1, heads * 64), F32)
    for head in range(heads):
        out = jnp.where(lane == head, scale[:, head : head + 1], out)
    return out


def split_heads(values, heads):
    lane = iota(values.shape, 1) >> 6
    zero = jnp.zeros_like(values)
    return jnp.concatenate([jnp.where(lane == head, values, zero) for head in range(heads)], axis=0)


def join_heads(stacked, heads):
    rows = stacked.shape[0] // heads
    lane = iota((rows, stacked.shape[1]), 1) >> 6
    out = stacked[:rows]
    for head in range(1, heads):
        out = jnp.where(lane == head, stacked[head * rows : (head + 1) * rows], out)
    return out


def rms(values, gain):
    scale = lax.rsqrt(jnp.mean(values * values, axis=-1, keepdims=True) + EPS)
    return (values * scale * gain).astype(BF)


def rms_back(values, gain, ct):
    scale = lax.rsqrt(jnp.mean(values * values, axis=-1, keepdims=True) + EPS)
    ct = ct * gain
    inner = jnp.mean(ct * values, axis=-1, keepdims=True)
    return scale * ct - values * (scale * scale * scale * inner)


def unit(values, block):
    return values * lax.rsqrt(head_sum(values * values, block) + EPS)


def unit_back(values, ct, block):
    scale = lax.rsqrt(head_sum(values * values, block) + EPS)
    return scale * ct - values * (scale * scale * scale * head_sum(ct * values, block))


def ordering(size, target):
    return zero_one(iota((size, target.shape[1]), 0) == target)


def merge_order():
    patch = iota((1, 256), 1)
    group = ((patch >> 3) & 2) + (patch & 1)
    return ordering(256, (group << 6) + ((patch >> 5) << 3) + ((patch >> 1) & 7))


def bits(count):
    return count.bit_length() - 1


def lanes_to_rows(values, rows, base):
    count, blocks = values.shape[0], values.shape[1] // 128
    for j in range(blocks):
        rows[pl.ds(base + j, count, stride=blocks), :] = values[:, 128 * j : 128 * j + 128]


def rows_to_lanes(rows, base, count, blocks):
    parts = [rows[pl.ds(base + j, count, stride=blocks), :] for j in range(blocks)]
    return jnp.concatenate(parts, axis=1)


def merged_spots():
    return [[32 * a + 16 * (group >> 1) + (group & 1) for a in range(8)] for group in range(4)]


def join_patches(groups, rows, base):
    for spots, group in zip(merged_spots(), groups):
        for a, spot in enumerate(spots):
            for half in range(2):
                part = group[8 * a : 8 * a + 8, 128 * half : 128 * half + 128]
                rows[pl.ds(base + 256 * half + spot, 8, stride=2), :] = part
    return jnp.concatenate([rows[base : base + 256], rows[base + 256 : base + 512]], axis=1)


def fine_project(
    tokens, gain, attend, scale, normed_out, raw_query_out, raw_key_out, query_out, key_out, value_out
):
    normed = rms(tokens[...].astype(F32), gain[...])
    normed_out[...] = normed
    block = head_block()
    triple = mm(normed, attend[...]).astype(BF)
    raw_query_out[...] = triple[:, :256]
    raw_key_out[...] = triple[:, 256:512]
    query = unit(triple[:, :256].astype(F32), block) * scale_lanes(scale, 4)
    query_out[...] = query.astype(BF)
    key_out[...] = unit(triple[:, 256:512].astype(F32), block).astype(BF)
    value_out[...] = triple[:, 512:]


def allowed_tiles(rank, keep):
    cell = iota((384, 128), 0)
    pick_row = zero_one((cell >> 4) + (16 * rank[0] - 3) == iota((384, 128), 1))
    kept = mm_nt(pick_row, keep[...].astype(F32).astype(BF))
    kept = jnp.where((iota((384, 16), 0) & 15) == iota((384, 16), 1), kept, 0.0)
    kept = jnp.sum(kept, axis=1, keepdims=True)
    spot, home = iota((256, 128), 0), iota((256, 128), 1)
    down = (spot >> 4) - (home >> 4) - 3
    across = (spot & 15) - (home & 15)
    inside = jnp.where((jnp.abs(down) <= 3) & (jnp.abs(across) <= 3), 1.0, 0.0)
    centre = jnp.where((down == 0) & (across == 0), 1.0, 0.0)
    return [inside * jnp.maximum(kept[at : at + 256], centre) for at in (0, 128)]


def fine_forward(
    rank,
    core,
    far,
    near_by,
    query,
    own_keys,
    own_value,
    tokens,
    gain,
    attend,
    keep,
    output,
    cotangent,
    merge,
    beside_out,
    raw_out,
    key_out,
    value_out,
    prob_out,
    attn_out,
    place_out,
    rows,
):
    del core
    is_even = (rank[0] & 1) == 0
    above = jnp.where(is_even, far[...].astype(F32), near_by[...].astype(F32))
    below = jnp.where(is_even, near_by[...].astype(F32), far[...].astype(F32))
    halo = jnp.concatenate([above, below], axis=0)
    normed = rms(halo, gain[...])
    beside_out[...] = normed
    beside = mm(normed, attend[:, 256:]).astype(BF)
    raw_out[...] = beside[:, :256]
    beside_keys = unit(beside[:, :256].astype(F32), head_block()).astype(BF)
    beside_value = beside[:, 256:]
    rest = jnp.zeros((32, 256), BF)
    keys = jnp.concatenate([beside_keys[:HALO], own_keys[...], beside_keys[HALO:], rest], axis=0)
    value = jnp.concatenate(
        [beside_value[:HALO], own_value[...], beside_value[HALO:], rest], axis=0
    )
    key_out[...] = keys
    value_out[...] = value
    tiles = allowed_tiles(rank, keep)
    parts = []
    for tile in range(2):
        at = 128 * tile
        allowed = jnp.concatenate([tiles[tile]] * 4, axis=1)
        score = mm_nt(keys[at : at + 256], split_heads(query[at : at + 128], 4))
        weight = jnp.exp(score) * allowed
        prob = (weight / jnp.sum(weight, axis=0, keepdims=True)).astype(BF)
        prob_out[tile] = prob
        parts.append(join_heads(mm_tn(prob, value[at : at + 256]), 4))
    attn = jnp.concatenate(parts, axis=0).astype(BF)
    attn_out[...] = attn
    mixed = (tokens[...].astype(F32) + mm(attn, output[...])).astype(BF)
    patches = mm(merge_order(), mixed).astype(BF)
    merged = mm(patches[:64], merge[:256])
    for group in range(1, 4):
        merged += mm(patches[64 * group : 64 * group + 64], merge[256 * group : 256 * group + 256])
    lanes_to_rows(jnp.concatenate([merged, cotangent[...].astype(F32)], axis=1), rows, 0)
    place_out[...] = rows[:512].astype(BF)


def coarse(place, gain, attend, scale, output, grad_out, back_out, rows, back_rows):
    rows[:512] = place[...].astype(F32)
    both = rows_to_lanes(rows, 0, 64, 8)
    merged, target = both[:, :512], both[:, 512:].astype(BF)
    block = head_block()
    lanes = scale_lanes(scale, 8)
    normed = rms(merged, gain[...])
    triple = mm(normed, attend[...]).astype(BF)
    query_raw, key_raw = triple[:, :512].astype(F32), triple[:, 512:1024].astype(F32)
    value = triple[:, 1024:]
    query = (unit(query_raw, block) * lanes).astype(BF)
    keys = unit(key_raw, block).astype(BF)
    ct_attn = mm_nt(target, output[...]).astype(BF)
    attns, ct_queries, ct_keys, ct_values = [], [], [], []
    for at in (0, 256):
        part = slice(at, at + 256)
        query_heads = split_heads(query[:, part], 4)
        weight = jnp.exp(mm_nt(keys[:, part], query_heads))
        prob = weight / jnp.sum(weight, axis=0, keepdims=True)
        prob_half = prob.astype(BF)
        attns.append(join_heads(mm_tn(prob_half, value[:, part]), 4).astype(BF))
        ct_heads = split_heads(ct_attn[:, part], 4)
        ct_prob = mm_nt(value[:, part], ct_heads)
        ct_score = prob * (ct_prob - jnp.sum(ct_prob * prob, axis=0, keepdims=True))
        ct_score = ct_score.astype(BF)
        ct_queries.append(join_heads(mm_tn(ct_score, keys[:, part]), 4))
        ct_keys.append(mm(ct_score, query_heads))
        ct_values.append(mm(prob_half, ct_heads))
    attn = jnp.concatenate(attns, axis=1)
    ct_query = jnp.concatenate(ct_queries, axis=1)
    ct_key = jnp.concatenate(ct_keys, axis=1)
    ct_value = jnp.concatenate(ct_values, axis=1).astype(BF)
    grad = mm_tn(attn, target)
    for part in range(4):
        rows[pl.ds(part, 512, stride=4), :] = grad[:, 128 * part : 128 * part + 128]
    grad_out[...] = rows[:2048].astype(BF)
    ct_triple = jnp.concatenate(
        [
            unit_back(query_raw, ct_query * lanes, block).astype(BF),
            unit_back(key_raw, ct_key, block).astype(BF),
            ct_value,
        ],
        axis=1,
    )
    ct_normed = mm_nt(ct_triple, attend[...]).astype(BF).astype(F32)
    ct_merged = target.astype(F32) + rms_back(merged, gain[...], ct_normed)
    lanes_to_rows(ct_merged, back_rows, 0)
    back_out[...] = back_rows[:256].astype(BF)


def fine_backward(
    core,
    back,
    grad_three,
    normed,
    raw_query,
    raw_key,
    query,
    normed_beside,
    raw_beside,
    keys,
    value,
    prob,
    attn,
    scale,
    output,
    merge,
    keep_out,
    send_out,
    above_out,
    below_out,
    mixed_out,
    ct_query_out,
    ct_key_out,
    ct_value_out,
    rows,
):
    block = head_block()
    rows[:256] = back[...].astype(F32)
    ct_merged = rows_to_lanes(rows, 0, 64, 4).astype(BF)
    groups = [mm_nt(ct_merged, merge[256 * group : 256 * group + 256]) for group in range(4)]
    ct_mixed = join_patches(groups, rows, 256).astype(BF)
    mixed_out[...] = ct_mixed
    ct_attn = mm_nt(ct_mixed, output[...]).astype(BF)
    ct_queries, ct_keys, ct_values = [], [], []
    for tile in range(2):
        at = 128 * tile
        ct_heads = split_heads(ct_attn[at : at + 128], 4)
        query_heads = split_heads(query[at : at + 128], 4)
        prob_half = prob[tile]
        wide = prob_half.astype(F32)
        ct_prob = mm_nt(value[at : at + 256], ct_heads)
        ct_score = wide * (ct_prob - jnp.sum(ct_prob * wide, axis=0, keepdims=True))
        ct_score = ct_score.astype(BF)
        ct_queries.append(join_heads(mm_tn(ct_score, keys[at : at + 256]), 4))
        ct_keys.append(mm(ct_score, query_heads))
        ct_values.append(mm(prob_half, ct_heads))
    both = []
    for at, parts, out in ((0, ct_keys, ct_key_out), (256, ct_values, ct_value_out)):
        first, second = parts
        middle = first[128:] + second[:128]
        own = jnp.concatenate([first[HALO:128], middle, second[128 : 128 + HALO]], axis=0)
        upper, lower = first[:HALO], second[128 + HALO : 128 + 2 * HALO]
        out[...] = own.astype(BF)
        above_out[:, at : at + 256] = upper.astype(BF)
        below_out[:, at : at + 256] = lower.astype(BF)
        both.append(jnp.concatenate([own, upper, lower], axis=0))
    ct_query = jnp.concatenate(ct_queries, axis=0) * scale_lanes(scale, 4)
    ct_query = unit_back(raw_query[...].astype(F32), ct_query, block).astype(BF)
    ct_query_out[...] = ct_query
    raw_keys = jnp.concatenate([raw_key[...], raw_beside[...]], axis=0).astype(F32)
    ct_key = unit_back(raw_keys, both[0], block).astype(BF)
    normed_all = jnp.concatenate([normed[...], normed_beside[...]], axis=0)
    grads = [
        mm_tn(normed[...], ct_query),
        mm_tn(normed_all, ct_key),
        mm_tn(normed_all, both[1].astype(BF)),
    ]
    last = mm_tn(attn[...], ct_mixed)
    for half in range(2):
        lanes = slice(128 * half, 128 * half + 128)
        for at, grad in enumerate(grads):
            rows[pl.ds(2 * at + half, 256, stride=6), :] = grad[:, lanes]
        rows[pl.ds(1536 + half, 256, stride=2), :] = last[:, lanes]
    own_even = core[0] == 0
    for pair in range(16):
        even = rows[128 * pair : 128 * pair + 64].astype(BF)
        odd = rows[128 * pair + 64 : 128 * pair + 128].astype(BF)
        at = 64 * pair
        keep_out[at : at + 64] = jnp.where(own_even, even, odd)
        send_out[at : at + 64] = jnp.where(own_even, odd, even)
        even = grad_three[128 * pair : 128 * pair + 64]
        odd = grad_three[128 * pair + 64 : 128 * pair + 128]
        at = 1024 + 64 * pair
        keep_out[at : at + 64] = jnp.where(own_even, even, odd)
        send_out[at : at + 64] = jnp.where(own_even, odd, even)


def fine_finish(
    from_above,
    from_below,
    ct_query,
    ct_key,
    ct_value,
    raw_key,
    ct_mixed,
    tokens,
    gain,
    attend,
    tokens_out,
    done_out,
):
    above, below = from_above[...].astype(F32), from_below[...].astype(F32)

    def with_edges(own, at):
        return jnp.concatenate(
            [
                own[:HALO].astype(F32) + above[:, at : at + 256],
                own[HALO : 256 - HALO].astype(F32),
                own[256 - HALO :].astype(F32) + below[:, at : at + 256],
            ],
            axis=0,
        ).astype(BF)

    key_total = with_edges(ct_key[...], 0).astype(F32)
    value_total = with_edges(ct_value[...], 256)
    ct_key_raw = unit_back(raw_key[...].astype(F32), key_total, head_block()).astype(BF)
    ct_triple = jnp.concatenate([ct_query[...], ct_key_raw, value_total], axis=1)
    ct_normed = mm_nt(ct_triple, attend[...]).astype(BF).astype(F32)
    own = tokens[...].astype(F32)
    total = ct_mixed[...].astype(F32) + rms_back(own, gain[...], ct_normed)
    tokens_out[...] = total.astype(BF)
    done_out[...] = jnp.zeros((8, 128), F32)


def add_pair(kept, sent, out, total, sems):
    copies = []
    for quarter in range(4):
        part = pl.ds(512 * quarter, 512)
        total[part] = (kept[part].astype(F32) + sent[part].astype(F32)).astype(BF)
        copy = pltpu.make_async_copy(total.at[part], out.at[part], sems.at[quarter])
        copy.start()
        copies.append(copy)
    for copy in copies:
        copy.wait()


def add_all(shares, done, out):
    del done
    total = [shares[at].astype(F32) for at in range(4)]
    for device in range(4, shares.shape[0]):
        total[device % 4] += shares[device].astype(F32)
    out[...] = (total[0] + total[1]) + (total[2] + total[3])


class Late:
    def __init__(self, copy, ref):
        self.copy, self.ref = copy, ref

    def wait(self):
        if self.copy is not None:
            self.copy.wait()
            self.copy = None

    def __getitem__(self, index):
        self.wait()
        return self.ref[index]


def split(values, *sizes):
    out, at = [], 0
    for size in sizes:
        out.append(values[at : at + size])
        at += size
    return out


def near(shape, dtype=BF):
    return pltpu.VMEM(shape, dtype)


def call(kernel, outs, *args, smem=0, scratch=(), cost=None):
    local = pl.BlockSpec(memory_space=pltpu.VMEM)
    scalar = pl.BlockSpec(memory_space=pltpu.SMEM)
    return pl.pallas_call(
        kernel,
        out_shape=outs,
        in_specs=[scalar] * smem + [local] * (len(args) - smem),
        scratch_shapes=scratch,
        out_specs=[local] * len(outs),
        compiler_params=pltpu.CompilerParams(vmem_limit_bytes=VMEM_BYTES),
        cost_estimate=cost,
    )(*args)


def fetch_and_call(kernel, outs, used, *args, cost=None):
    count = len(args)
    local = pl.BlockSpec(memory_space=pltpu.VMEM)
    hbm = pl.BlockSpec(memory_space=pltpu.HBM)

    def run(*refs):
        sources, held, rest = refs[:count], refs[count : 2 * count], refs[2 * count :]
        sems = rest[-1]
        late = []
        for at in range(count):
            copy = pltpu.make_async_copy(sources[at], held[at], sems.at[at])
            copy.start()
            late.append(Late(copy, held[at]))
        kernel(*late[:used], *rest[:-1])
        for one in late:
            one.wait()

    return pl.pallas_call(
        run,
        out_shape=[near(arg.shape, arg.dtype) for arg in args] + outs,
        in_specs=[hbm] * count,
        out_specs=[local] * (count + len(outs)),
        scratch_shapes=[pltpu.SemaphoreType.DMA((count,))],
        compiler_params=pltpu.CompilerParams(vmem_limit_bytes=VMEM_BYTES),
        cost_estimate=cost,
    )(*[pltpu.with_memory_space_constraint(arg, pltpu.HBM) for arg in args])


def body(
    tokens,
    keep_mask,
    gain_two,
    attend_two,
    scale_two,
    output_two,
    merge_weight,
    gain_three,
    attend_three,
    scale_three,
    output_three,
    cotangent,
):
    count = lax.axis_size("rows")
    to_next = [(i, i + 1) for i in range(count - 1)]
    to_last = [(i + 1, i) for i in range(count - 1)]
    own = tokens.reshape(256, 256)
    is_even = (lax.axis_index("rows") & 1) == 0
    top, bottom = own[:HALO], own[256 - HALO :]
    pairs = [(at, ((at + 1) ^ 1) - 1) for at in range(1, count - 1)]
    far = lax.ppermute(jnp.where(is_even, top, bottom), "rows", pairs)
    pairs = [(at, at ^ 1) for at in range(count)]
    near_by = lax.ppermute(jnp.where(is_even, bottom, top), "rows", pairs)
    rank = lax.axis_index("rows").astype(jnp.int32).reshape(1)
    core = (lax.axis_index("frames") & 1).astype(jnp.int32).reshape(1)
    square = (256, 256)
    (
        (own, gain_two, attend_two, scale_two, keep, output_two, cot, merge_weight),
        three,
        (normed, raw_query, raw_key, query, own_keys, own_value),
    ) = split(
        fetch_and_call(
            fine_project,
            [near(square)] * 6,
            4,
            own,
            gain_two.reshape(1, 256),
            attend_two,
            scale_two.reshape(1, 4),
            keep_mask.reshape(128, 16).T,
            output_two,
            cotangent.reshape(64, 512),
            merge_weight,
            gain_three.reshape(1, 512),
            attend_three,
            scale_three.reshape(1, 8),
            output_three,
            cost=pl.CostEstimate(flops=170_000_000, bytes_accessed=5_000_000, transcendentals=0),
        ),
        8,
        4,
        6,
    )
    normed_beside, raw_beside, keys, value, prob, attn, place = call(
        fine_forward,
        [
            near((96, 256)),
            near((96, 256)),
            near((384, 256)),
            near((384, 256)),
            near((2, 256, 512)),
            near(square),
            jax.ShapeDtypeStruct((512, 128), BF),
        ],
        rank,
        core,
        far,
        near_by,
        query,
        own_keys,
        own_value,
        own,
        gain_two,
        attend_two,
        keep,
        output_two,
        cot,
        merge_weight,
        smem=2,
        scratch=[pltpu.VMEM((512 + SPARE, 128), F32)],
    )
    place = lax.all_to_all(place.reshape(64, 8, 128), "frames", 0, 0, tiled=True)
    grad_three, back = call(
        coarse,
        [near((2048, 128)), jax.ShapeDtypeStruct((256, 128), BF)],
        place.reshape(512, 128),
        *three,
        scratch=[pltpu.VMEM((2048 + SPARE, 128), F32), pltpu.VMEM((256 + SPARE, 128), F32)],
    )
    back = lax.all_to_all(back.reshape(64, 4, 128), "frames", 0, 0, tiled=True)
    kept, sent, up, down, ct_mixed, ct_query, ct_key, ct_value = call(
        fine_backward,
        [
            near((2048, 128)),
            jax.ShapeDtypeStruct((2048, 128), BF),
            jax.ShapeDtypeStruct((HALO, 512), BF),
            jax.ShapeDtypeStruct((HALO, 512), BF),
            near(square),
            near(square),
            near(square),
            near(square),
        ],
        core,
        back.reshape(256, 128),
        grad_three,
        normed,
        raw_query,
        raw_key,
        query,
        normed_beside,
        raw_beside,
        keys,
        value,
        prob,
        attn,
        scale_two,
        output_two,
        merge_weight,
        smem=1,
        scratch=[pltpu.VMEM((2048 + SPARE, 128), F32)],
    )
    pairs = [(i, i ^ 1) for i in range(lax.axis_size("frames"))]
    sent = lax.ppermute(sent, "frames", pairs)
    from_below = lax.ppermute(up, "rows", to_last)
    from_above = lax.ppermute(down, "rows", to_next)
    tokens_grad, done = call(
        fine_finish,
        [jax.ShapeDtypeStruct(square, BF), near((8, 128), F32)],
        from_above,
        from_below,
        ct_query,
        ct_key,
        ct_value,
        raw_key,
        ct_mixed,
        own,
        gain_two,
        attend_two,
        cost=pl.CostEstimate(flops=170_000_000, bytes_accessed=2_000_000, transcendentals=0),
    )
    shares = pl.pallas_call(
        add_pair,
        out_shape=jax.ShapeDtypeStruct((2048, 128), BF),
        in_specs=[pl.BlockSpec(memory_space=pltpu.VMEM)] * 2,
        out_specs=pl.BlockSpec(memory_space=pltpu.HBM),
        scratch_shapes=[pltpu.VMEM((2048, 128), BF), pltpu.SemaphoreType.DMA((4,))],
        compiler_params=pltpu.CompilerParams(vmem_limit_bytes=VMEM_BYTES),
    )(kept, sent)
    every = lax.axis_size("frames") * count
    groups = [[at for at in range(every) if at // count % 2 == own] for own in (0, 1)]
    shares = lax.all_to_all(
        shares.reshape(every // 2, 8, 128),
        ("frames", "rows"),
        0,
        0,
        tiled=True,
        axis_index_groups=groups,
    )
    (total,) = call(add_all, [jax.ShapeDtypeStruct((8, 128), F32)], shares, done)
    return (tokens_grad.reshape(tokens.shape), total.reshape(1, 1024))


def solution(mesh):
    return jax.shard_map(
        body,
        mesh=mesh,
        in_specs=(
            P("frames", "rows", None, None),
            P("frames", None, None),
            P(),
            P(),
            P(),
            P(),
            P(),
            P(),
            P(),
            P(),
            P(),
            P("frames", "rows", None, None),
        ),
        out_specs=(P("frames", "rows", None, None), P(("frames", "rows"), None)),
        check_vma=False,
    )
```
